1024 devices in a mesh: tile: 64 (over z, core), band: 16 (over x, y).
Axes of the slice: x: 4, y: 4, z: 32, core: 2. Of those that a mesh axis runs over, the one named last changes fastest.
Arguments:
- ocean_velocity: float32 [2, 8, 256, 8192], P(None, None, 'band', 'tile'), may hold values from -6 to 6
- ocean_wet: int32 [256, 8192], P('band', 'tile'), may hold values 0 or 1
- coriolis: float32 [256], P('band'), may hold values from -2 to 2
- spectrum: float32 [128, 1024, 1296], P('band', 'tile'), may hold values from 0.05 to 2
- group_speed: float32 [36], replicated, may hold values from 0.5 to 2
- source_matrix: bfloat16 [1296, 1296], replicated, may hold values from -0.15625 to 0.15625
- moments: float32 [4, 1296], replicated, may hold values from -0.15625 to 0.15625
- o2w_rows: int32 [64, 16, 64, 2], P('tile', 'band'), may hold values from 0 to 31
- ocean_to_wave_index: int32 [4, 128, 1024], P(None, 'band', 'tile'), may hold values from 0 to 16383
- o2w_weight: int32 [4, 128, 1024], P(None, 'band', 'tile'), may hold values from 1 to 8
- w2o_rows: int32 [64, 16, 64, 1], P('tile', 'band'), may hold values from 0 to 1
- wave_to_ocean_index: int32 [4, 256, 8192], P(None, 'band', 'tile'), may hold values from 0 to 8191
- wave_to_ocean_weight: int32 [4, 256, 8192], P(None, 'band', 'tile'), may hold values from 1 to 8
Outputs:
- ocean_next: float32 [2, 8, 256, 8192], P(None, None, 'band', 'tile')
- spectrum_next: float32 [128, 1024, 1296], P('band', 'tile')
The draws below stay inside these ranges and needn't reach their ends.
Inputs may be any that keep to these rules, and one draw needn't show every extreme that they name: `o2w_rows`: entries below 16 name a row of the sending ocean block; larger entries mark an empty slot. `ocean_to_wave_index`: index into the wave block's received buffer of 64 x 2 x 128 entries. `w2o_rows`: entries below 1 name a list row of the sending wave block; larger entries mark an empty slot. `wave_to_ocean_index`: index into the ocean block's received buffer of 64 x 1 x 128 entries.
All inputs are finite; a program needn't handle non-finite values. No bound on the sum of `ocean_wet` on one device may be relied on, other than what follows from the above.
Results may differ from the reference program's by a relative error of at most 0.001.
Values sent between devices are 32-bit elements; how exact they have to be, the bound alone decides.
A program may use at most 64 MiB of HBM per device.

```python
import math
import jax
import jax.numpy as jnp
from jax import lax

NDIR = 36
NFREQ = 36
LIST_ROW_LENGTH = 128
LEV = 8
BLOCK_ROWS = 16
BLOCK_WAVE_ROWS = 8
BLOCK_WAVE_COLS = 16
OCEAN_WAVE_SLOT = 2
WAVE_OCEAN_SLOT = 1
ENTRY_COUNT = 4
WSTEPS = 2
TILE_COUNT = 64
BAND_COUNT = 16
NBIN = 1296
WAVE_LIST_ROWS = 1
OCEAN_ROWS = 256
OCEAN_COLUMNS = 8192
WAVE_ROWS = 128
WAVE_COLUMNS = 1024


def plant(result, key, smallest, high):
    extent = result.shape
    place = [jax.random.randint(jax.random.fold_in(key, axis), (), 0, extent[axis]) for axis in range(len(extent))]
    result = result.at[tuple(place)].set(smallest)
    longest = extent.index(max(extent))
    place[longest] = (place[longest] + 1) % extent[longest]
    return result.at[tuple(place)].set(high)


def steps_of(own_key, dims, split, smallest, top_value):
    factor_of, own = 1.0, jax.random.fold_in(own_key, 6)
    for position, shards_of in split:
        steps = jnp.exp(jax.random.uniform(jax.random.fold_in(own, position), (shards_of,), jnp.float32, smallest / len(split), top_value / len(split)))
        factor_of = factor_of * jnp.repeat(steps, dims[position] // shards_of).reshape([-1 if axis == position else 1 for axis in range(len(dims))])
    return factor_of


def bell_draw(stream_key, shape, width, bound, cuts=(), kind=jnp.bfloat16):
    result = jax.random.normal(stream_key, shape, jnp.float32) * width
    if len(cuts) > 0:
        result = steps_of(stream_key, shape, cuts, -0.22, 0.18) * result
    return jnp.clip(result, min=-bound, max=bound).astype(kind)


def setup_inputs(seed: int = 0) -> dict:
    key_list = jax.random.split(jax.random.key(seed), 14)
    ocean_velocity = bell_draw(key_list[0], (2, LEV, OCEAN_ROWS, OCEAN_COLUMNS), 1.0, 6.0, ((2, 16), (3, 64)), jnp.float32)
    ocean_wet = plant((jax.random.randint(key_list[1], (OCEAN_ROWS, OCEAN_COLUMNS), 0, 10) < 9).astype(jnp.int32), jax.random.fold_in(key_list[1], 1), 0, 1)
    coriolis = jnp.clip(jax.random.uniform(key_list[2], (OCEAN_ROWS,), jnp.float32, -2.0, 2.0) * steps_of(key_list[2], (OCEAN_ROWS,), ((0, 16),), -0.4, 0.0), -2.0, 2.0)
    spectrum = jnp.clip(jnp.exp(math.log(2.0) - 3.6888794 * jax.random.uniform(key_list[3], (WAVE_ROWS, WAVE_COLUMNS, NBIN), jnp.float32) ** steps_of(key_list[3], (WAVE_ROWS, WAVE_COLUMNS, NBIN), ((0, 16), (1, 64)), -0.2, 0.2)), 0.05, 2.0)
    group_speed = jnp.clip(jnp.exp(jax.random.uniform(key_list[4], (NFREQ,), jnp.float32, math.log(0.5), math.log(2.0))), 0.5, 2.0)
    source_matrix = bell_draw(key_list[5], (NBIN, NBIN), NBIN ** -0.5, 0.15625)
    moments = bell_draw(key_list[6], (4, NBIN), NBIN ** -0.5, 0.15625, (), jnp.float32)
    o2w_rows = plant(jax.random.randint(key_list[7], (TILE_COUNT, BAND_COUNT, TILE_COUNT, OCEAN_WAVE_SLOT), 0, 2 * BLOCK_ROWS), jax.random.fold_in(key_list[7], 1), 0, (2 * BLOCK_ROWS) - 1).astype(jnp.int32)
    ocean_to_wave_index = plant(jax.random.randint(key_list[8], (ENTRY_COUNT, WAVE_ROWS, WAVE_COLUMNS), 0, TILE_COUNT * OCEAN_WAVE_SLOT * LIST_ROW_LENGTH), jax.random.fold_in(key_list[8], 1), 0, (TILE_COUNT * OCEAN_WAVE_SLOT * LIST_ROW_LENGTH) - 1).astype(jnp.int32)
    o2w_weight = plant(jax.random.randint(key_list[9], (ENTRY_COUNT, WAVE_ROWS, WAVE_COLUMNS), 1, 9), jax.random.fold_in(key_list[9], 1), 1, 8).astype(jnp.int32)
    w2o_rows = plant(jax.random.randint(key_list[10], (TILE_COUNT, BAND_COUNT, TILE_COUNT, WAVE_OCEAN_SLOT), 0, 2 * WAVE_LIST_ROWS), jax.random.fold_in(key_list[10], 1), 0, (2 * WAVE_LIST_ROWS) - 1).astype(jnp.int32)
    wave_to_ocean_index = plant(jax.random.randint(key_list[11], (ENTRY_COUNT, OCEAN_ROWS, OCEAN_COLUMNS), 0, TILE_COUNT * WAVE_OCEAN_SLOT * LIST_ROW_LENGTH), jax.random.fold_in(key_list[11], 1), 0, (TILE_COUNT * WAVE_OCEAN_SLOT * LIST_ROW_LENGTH) - 1).astype(jnp.int32)
    wave_to_ocean_weight = plant(jax.random.randint(key_list[12], (ENTRY_COUNT, OCEAN_ROWS, OCEAN_COLUMNS), 1, 9), jax.random.fold_in(key_list[12], 1), 1, 8).astype(jnp.int32)
    return {"ocean_velocity": ocean_velocity, "ocean_wet": ocean_wet, "coriolis": coriolis, "spectrum": spectrum, "group_speed": group_speed, "source_matrix": source_matrix, "moments": moments, "o2w_rows": o2w_rows, "ocean_to_wave_index": ocean_to_wave_index, "o2w_weight": o2w_weight, "w2o_rows": w2o_rows, "wave_to_ocean_index": wave_to_ocean_index, "wave_to_ocean_weight": wave_to_ocean_weight}


DT_OCEAN = 0.2
VISCOSITY = 0.5
VERT_FRICTION = 0.5
STRESS_COEFF = 1.0
DT_WAVE = 0.1
DT_SOURCE = 0.3


def bin_speeds(group_speed):
    angle = (jnp.arange(NDIR, dtype=jnp.float32) + 0.5) * (2.0 * math.pi / NDIR)
    speed_x = (jnp.cos(angle)[:, None] * group_speed[None, :]).reshape(NDIR * NFREQ)
    speed_y = (jnp.sin(angle)[:, None] * group_speed[None, :]).reshape(NDIR * NFREQ)
    return speed_x, speed_y


def advance(padded, current_x, current_y, speed_x, speed_y, source_matrix):
    center = padded[1:-1, 1:-1]
    west_side = padded[1:-1, :-2]
    east_side = padded[1:-1, 2:]
    south_side = padded[:-2, 1:-1]
    north_side = padded[2:, 1:-1]
    flow_x = speed_x + current_x[:, :, None]
    flow_y = speed_y + current_y[:, :, None]
    change = (jnp.maximum(flow_x, 0.0) * (center - west_side) + jnp.minimum(flow_x, 0.0) * (east_side - center)
              + jnp.maximum(flow_y, 0.0) * (center - south_side) + jnp.minimum(flow_y, 0.0) * (north_side - center))
    moved = center - DT_WAVE * change
    rounded = moved.astype(jnp.bfloat16)
    source = jnp.dot(rounded.reshape(-1, moved.shape[2]), source_matrix, preferred_element_type=jnp.float32)
    return moved + DT_SOURCE * source.reshape(moved.shape)


def weighted_pick(buffer, index, weight):
    values = buffer[:, index]
    factor = weight.astype(jnp.float32)
    return jnp.sum(values * factor[None], axis=1) / jnp.sum(factor, axis=0)


def ocean_update(velocity, padded, wet, coriolis, forcing_field):
    laplace = (padded[:, :, :-2, 1:-1] + padded[:, :, 2:, 1:-1] + padded[:, :, 1:-1, :-2]
               + padded[:, :, 1:-1, 2:] - 4.0 * velocity)
    above = jnp.concatenate([velocity[:, :1], velocity[:, :-1]], axis=1)
    below = jnp.concatenate([velocity[:, 1:], velocity[:, -1:]], axis=1)
    vertical = above - 2.0 * velocity + below
    rotation = coriolis[:, None]
    turning = jnp.stack([rotation * velocity[1], -rotation * velocity[0]])
    tendency = VISCOSITY * laplace + VERT_FRICTION * vertical + turning
    surface_layer = jnp.stack([STRESS_COEFF * forcing_field[0] + rotation * forcing_field[3],
                         STRESS_COEFF * forcing_field[1] - rotation * forcing_field[2]])
    tendency = tendency.at[:, 0].add(surface_layer)
    return wet.astype(jnp.float32) * (velocity + DT_OCEAN * tendency)


def remap(values, row_list, index, weight):
    count = values.shape[3]
    padded = jnp.concatenate([values, jnp.zeros(values.shape[:3] + (1, values.shape[4]), values.dtype)], axis=3)
    chosen = jnp.minimum(row_list, count).transpose(1, 0, 2, 3)

    def one_band(items):
        band_values, band_rows, band_index, band_weight = items
        picked = jax.vmap(lambda source_part, row_choice: jnp.take(source_part, row_choice, axis=1))(band_values, band_rows)
        buffers = picked.transpose(2, 1, 0, 3, 4).reshape(picked.shape[2], picked.shape[1], -1)
        return jax.vmap(weighted_pick)(buffers, band_index, band_weight)

    return lax.map(one_band, (padded, chosen, index, weight))


def wave_step(field, currents, speed_x, speed_y, source_matrix):
    padded = jnp.pad(field, ((1, 1), (1, 1), (0, 0)))

    def one_band(number):
        start = (number * BLOCK_WAVE_ROWS).astype(jnp.int32)
        block = lax.dynamic_slice_in_dim(padded, start, BLOCK_WAVE_ROWS + 2, 0)
        east_flow = lax.dynamic_slice_in_dim(currents[0], start, BLOCK_WAVE_ROWS, 0)
        north_flow = lax.dynamic_slice_in_dim(currents[1], start, BLOCK_WAVE_ROWS, 0)
        return advance(block, east_flow, north_flow, speed_x, speed_y, source_matrix)

    block_list = lax.map(one_band, jnp.arange(BAND_COUNT, dtype=jnp.int32))
    return block_list.reshape(WAVE_ROWS, WAVE_COLUMNS, NBIN)


def reference(ocean_velocity, ocean_wet, coriolis, spectrum, group_speed, source_matrix, moments,
              o2w_rows, ocean_to_wave_index, o2w_weight, w2o_rows, wave_to_ocean_index, wave_to_ocean_weight):
    surface_layer = ocean_velocity[:, 0].reshape(2, BAND_COUNT, BLOCK_ROWS, TILE_COUNT, LIST_ROW_LENGTH).transpose(1, 3, 0, 2, 4)
    pick_index = ocean_to_wave_index.reshape(ENTRY_COUNT, BAND_COUNT, BLOCK_WAVE_ROWS, TILE_COUNT, BLOCK_WAVE_COLS).transpose(1, 3, 0, 2, 4).reshape(BAND_COUNT, TILE_COUNT, ENTRY_COUNT, BLOCK_WAVE_ROWS * BLOCK_WAVE_COLS)
    pick_weight = o2w_weight.reshape(ENTRY_COUNT, BAND_COUNT, BLOCK_WAVE_ROWS, TILE_COUNT, BLOCK_WAVE_COLS).transpose(1, 3, 0, 2, 4).reshape(BAND_COUNT, TILE_COUNT, ENTRY_COUNT, BLOCK_WAVE_ROWS * BLOCK_WAVE_COLS)
    currents = remap(surface_layer, o2w_rows, pick_index, pick_weight)
    currents = currents.reshape(BAND_COUNT, TILE_COUNT, 2, BLOCK_WAVE_ROWS, BLOCK_WAVE_COLS).transpose(2, 0, 3, 1, 4).reshape(2, WAVE_ROWS, WAVE_COLUMNS)
    speed_x, speed_y = bin_speeds(group_speed)
    spectrum_now = spectrum
    for step in range(WSTEPS):
        spectrum_now = wave_step(spectrum_now, currents, speed_x, speed_y, source_matrix)
    total_sums = jnp.einsum('yxb,qb->qyx', spectrum_now, moments, precision=lax.Precision.HIGHEST)
    block_list = total_sums.reshape(4, BAND_COUNT, BLOCK_WAVE_ROWS, TILE_COUNT, BLOCK_WAVE_COLS).transpose(1, 3, 0, 2, 4).reshape(BAND_COUNT, TILE_COUNT, 4, WAVE_LIST_ROWS, LIST_ROW_LENGTH)
    return_index = wave_to_ocean_index.reshape(ENTRY_COUNT, BAND_COUNT, BLOCK_ROWS, TILE_COUNT, LIST_ROW_LENGTH).transpose(1, 3, 0, 2, 4).reshape(BAND_COUNT, TILE_COUNT, ENTRY_COUNT, BLOCK_ROWS * LIST_ROW_LENGTH)
    return_weight = wave_to_ocean_weight.reshape(ENTRY_COUNT, BAND_COUNT, BLOCK_ROWS, TILE_COUNT, LIST_ROW_LENGTH).transpose(1, 3, 0, 2, 4).reshape(BAND_COUNT, TILE_COUNT, ENTRY_COUNT, BLOCK_ROWS * LIST_ROW_LENGTH)
    forcing_field = remap(block_list, w2o_rows, return_index, return_weight)
    forcing_field = forcing_field.reshape(BAND_COUNT, TILE_COUNT, 4, BLOCK_ROWS, LIST_ROW_LENGTH).transpose(2, 0, 3, 1, 4).reshape(4, OCEAN_ROWS, OCEAN_COLUMNS)
    padded = jnp.pad(ocean_velocity, ((0, 0), (0, 0), (1, 1), (1, 1)))
    ocean_next = ocean_update(ocean_velocity, padded, ocean_wet, coriolis, forcing_field)
    return ocean_next, spectrum_now
```

```python
import functools
import math

import jax
import jax.numpy as jnp
import numpy as np
from jax import lax
from jax.experimental import pallas as pl
from jax.experimental.pallas import tpu as pltpu
from jax.sharding import PartitionSpec as P

NDIR = 36
NFREQ = 36
DT_OCEAN = 0.2
VISCOSITY = 0.5
VERT_FRICTION = 0.5
STRESS_COEFF = 1.0
DT_WAVE = 0.1
DT_SOURCE = 0.3

LANES = 128
MESH = pl.DeviceIdType.MESH
HIGHEST = lax.Precision.HIGHEST


def chunks(total, size):
    return [(start, min(start + size, total)) for start in range(0, total, size)]


def lane_pick(table, index):
    return jnp.take_along_axis(table, index, axis=1, mode="promise_in_bounds")


def kernel(
    tiles,
    bands,
    group,
    ocean_h, wet_h, coriolis_h, spectrum_h, speed_h, source_h, moments_h,
    o2w_rows_h, o2w_index_h, o2w_weight_h, w2o_rows_h, w2o_index_h, w2o_weight_h,
    wheel_h, wheel_index_h,
    ocean_out, spectrum_out,
    ocean, wet, coriolis, first, speed, source, moments,
    o2w_rows, o2w_index, o2w_weight, w2o_index, w2o_weight, wheel, wheel_index,
    outgoing, incoming, marks, totals,
    edge_w0, edge_e0, halo_w0, halo_e0, edge_w1, edge_e1, halo_w1, halo_e1,
    row_lo, row_hi, halo_lo, halo_hi, column_w, column_e, arrived_w, arrived_e,
    second, moved, rounded, leftover, speed_x, speed_y, flow_x, flow_y,
    halo_column, pad_small, pad_rows, pad_index, pad_moments, moments_t, mixed_t, mark_lanes,
    ocean_new, spectrum_new,
    load_sem, send_sem, recv_sem,
):
    tile, band = lax.axis_index("tile"), lax.axis_index("band")
    groups = tiles // group
    my_group, my_place = tile // group, tile % group
    east, west = lax.rem(tile + 1, tiles), lax.rem(tile + tiles - 1, tiles)
    north, south = lax.rem(band + 1, bands), lax.rem(band + bands - 1, bands)
    bins = first.shape[2]
    layers = ocean.shape[0]
    levels = layers // 2

    loads = [
        (ocean_h, ocean.at[:, 8:24, :]), (o2w_rows_h, o2w_rows), (spectrum_h, first.at[1:9, 8:24, :]),
        (w2o_rows_h, marks.at[my_place * groups + my_group]), (moments_h, moments), (source_h, source),
        (o2w_index_h, o2w_index), (o2w_weight_h, o2w_weight), (speed_h, speed), (wheel_h, wheel),
        (wheel_index_h, wheel_index), (wet_h, wet), (coriolis_h, coriolis), (w2o_index_h, w2o_index),
        (w2o_weight_h, w2o_weight),
    ]
    loads = [pltpu.make_async_copy(s, d, load_sem.at[i]) for i, (s, d) in enumerate(loads)]
    for load in loads:
        load.start()

    barrier = pltpu.get_barrier_semaphore()

    def greet(step, carry):
        pl.semaphore_signal(
            barrier, inc=1, device_id={"tile": lax.rem(tile + step, tiles)}, device_id_type=MESH
        )
        return carry

    lax.fori_loop(1, tiles, greet, 0)
    for other in (south, north):
        pl.semaphore_signal(barrier, inc=1, device_id={"band": other}, device_id_type=MESH)

    loads[0].wait()
    loads[1].wait()
    pad_rows[...] = jnp.zeros_like(pad_rows)
    pad_rows[0:2, 0:tiles] = o2w_rows[...]
    wanted = jnp.transpose(pad_rows[...].astype(jnp.float32))
    for slot in range(2):
        row = jnp.broadcast_to(wanted[0:tiles, slot : slot + 1], (tiles, LANES))
        east_part = jnp.zeros((tiles, LANES), jnp.float32)
        north_part = east_part
        for r in range(16):
            here = row == float(r)
            east_part = jnp.where(here, ocean[0, 8 + r : 9 + r, :], east_part)
            north_part = jnp.where(here, ocean[levels, 8 + r : 9 + r, :], north_part)
        outgoing[:, 2 * slot, :] = east_part
        outgoing[:, 2 * slot + 1, :] = north_part
    pl.semaphore_wait(barrier, tiles + 1)

    keep = pltpu.make_async_copy(outgoing.at[tile], incoming.at[tile], recv_sem.at[0])
    keep.start()

    def give(step, carry):
        half = (step + 1) // 2
        reach = tiles // 2 + half * (1 - 2 * (step % 2))
        target = lax.rem(tile + reach, tiles)
        pltpu.make_async_remote_copy(
            src_ref=outgoing.at[target], dst_ref=incoming.at[tile], send_sem=send_sem.at[0],
            recv_sem=recv_sem.at[0], device_id={"tile": target}, device_id_type=MESH,
        ).start()
        return carry

    lax.fori_loop(0, tiles - 1, give, 0)

    def send(index, src, dst, where):
        copy = pltpu.make_async_remote_copy(
            src_ref=src, dst_ref=dst, send_sem=send_sem.at[index], recv_sem=recv_sem.at[index],
            device_id=where, device_id_type=MESH,
        )
        copy.start()
        return copy

    def spread_far(index, ref):
        own = my_place * groups + my_group
        for step in range(1, groups):
            target = lax.rem(my_group + step, groups) * group + my_place
            send(index, ref.at[own], ref.at[own], {"tile": target})

    def spread_near(index, ref):
        own = pl.ds(my_place * groups, groups)
        for step in range(1, group):
            target = my_group * group + lax.rem(my_place + step, group)
            send(index, ref.at[own], ref.at[own], {"tile": target})

    def await_blocks(sem, ref, count):
        part = ref.at[pl.ds(0, count)]
        pltpu.make_async_copy(part, part, sem).wait()

    def send_edges(base, field, edge_w, edge_e, halo_w, halo_e):
        edge_w[...] = field[1:9, 8, :]
        edge_e[...] = field[1:9, 23, :]
        return [
            send(base, field.at[1, 8:24, :], field.at[9, 8:24, :], {"band": south}),
            send(base + 1, field.at[8, 8:24, :], field.at[0, 8:24, :], {"band": north}),
            send(base + 2, edge_w, halo_e, {"tile": west}),
            send(base + 3, edge_e, halo_w, {"tile": east}),
        ]

    def place_edges(copies, field, halo_w, halo_e):
        for copy in copies:
            copy.wait_recv()
        field[1:9, 7, :] = halo_w[...] * jnp.where(tile == 0, 0.0, 1.0)
        field[1:9, 24, :] = halo_e[...] * jnp.where(tile == tiles - 1, 0.0, 1.0)

        @pl.when(band == 0)
        def _():
            field[0, 8:24, :] = jnp.zeros((16, bins), jnp.float32)

        @pl.when(band == bands - 1)
        def _():
            field[9, 8:24, :] = jnp.zeros((16, bins), jnp.float32)

    loads[2].wait()
    edges = send_edges(1, first, edge_w0, edge_e0, halo_w0, halo_e0)
    loads[3].wait()
    spread_far(5, marks)

    row_lo[...] = ocean[:, 8, :]
    row_hi[...] = ocean[:, 23, :]
    flat = ocean[:, 8:24, :].reshape(layers * 16, LANES)
    turned = jnp.transpose(flat)
    column_w[...] = jnp.broadcast_to(turned[0:1, :], column_w.shape)
    column_e[...] = jnp.broadcast_to(turned[LANES - 1 : LANES, :], column_e.shape)
    ocean_edges = [
        send(7, row_lo, halo_hi, {"band": south}),
        send(8, row_hi, halo_lo, {"band": north}),
    ]
    ocean_edges += [
        send(9, column_w, arrived_e, {"tile": west}),
        send(10, column_e, arrived_w, {"tile": east}),
    ]

    for load in (4, 8, 9, 10):
        loads[load].wait()
    pad_small[...] = jnp.zeros_like(pad_small)
    pad_small[0:1, 0:NFREQ] = speed[...]
    speeds = jnp.broadcast_to(pad_small[0:1, :], (8, LANES))
    for lo, hi in chunks(speed_x.shape[1], LANES):
        picked = lane_pick(speeds, wheel_index[:, lo:hi])
        speed_x[:, lo:hi] = picked * wheel[0:1, lo:hi]
        speed_y[:, lo:hi] = picked * wheel[1:2, lo:hi]

    pad_moments[...] = jnp.zeros_like(pad_moments)
    pad_moments[0:4, 0:bins] = moments[...]
    for lo, hi in chunks(pad_moments.shape[1], LANES):
        top = min(hi, bins)
        part = jnp.transpose(pad_moments[:, lo:hi])
        high = part.astype(jnp.bfloat16)
        low = part - high.astype(jnp.float32)
        both = high.astype(jnp.float32) + pltpu.roll(low, 8, 1)
        moments_t[lo:top, :] = both[0 : top - lo].astype(jnp.bfloat16)
    loads[5].wait()
    lane = lax.broadcasted_iota(jnp.int32, (144, LANES), 1)

    def mix(step, carry):
        rows = pl.ds(pl.multiple_of(step * 144, 144), 144)
        mixed = jnp.dot(source[rows, :], moments_t[...], preferred_element_type=jnp.float32)
        own = moments_t[rows, :].astype(jnp.float32)
        full = own + DT_SOURCE * mixed
        full = jnp.where(lane < 8, full + pltpu.roll(full, LANES - 8, 1), 0.0)
        high = full.astype(jnp.bfloat16)
        low = full - high.astype(jnp.float32)
        both = high.astype(jnp.float32) + pltpu.roll(low, 8, 1)
        mixed_t[rows, :] = both.astype(jnp.bfloat16)
        return carry

    lax.fori_loop(0, bins // 144, mix, 0)

    await_blocks(recv_sem.at[5], marks, groups - 1)
    spread_near(6, marks)

    for copy in ocean_edges:
        copy.wait_recv()
    loads[11].wait()
    loads[12].wait()
    ocean[:, 7, :] = halo_lo[...] * jnp.where(band == 0, 0.0, 1.0)
    ocean[:, 24, :] = halo_hi[...] * jnp.where(band == bands - 1, 0.0, 1.0)
    halo_column[...] = jnp.zeros_like(halo_column)
    halo_column[0, 0:8, :] = arrived_w[...]
    halo_column[1, LANES - 8 : LANES, :] = arrived_e[...]
    column_from_w = jnp.transpose(halo_column[0]) * jnp.where(tile == 0, 0.0, 1.0)
    column_from_e = jnp.transpose(halo_column[1]) * jnp.where(tile == tiles - 1, 0.0, 1.0)
    spot = lax.broadcasted_iota(jnp.int32, (16, LANES), 1)
    line = lax.broadcasted_iota(jnp.int32, (16, LANES), 0)
    pad_small[...] = jnp.zeros_like(pad_small)
    pad_small[0:1, 0:16] = coriolis[...]
    rotation = jnp.sum(
        jnp.where(spot == line, jnp.broadcast_to(pad_small[0:1, :], (16, LANES)), 0.0),
        axis=1, keepdims=True,
    )
    rotation = jnp.broadcast_to(rotation, (16, LANES))
    wet_now = wet[...].astype(jnp.float32)
    for level in range(levels):
        for part in range(2):
            n = part * levels + level
            here = ocean[n, 8:24, :]
            lanes_w = jnp.where(spot == 0, column_from_w[16 * n : 16 * n + 16], pltpu.roll(here, 1, 1))
            lanes_e = jnp.where(
                spot == LANES - 1, column_from_e[16 * n : 16 * n + 16], pltpu.roll(here, LANES - 1, 1)
            )
            laplace = ocean[n, 7:23, :] + ocean[n, 9:25, :] + lanes_w + lanes_e - 4.0 * here
            above = ocean[n - 1 if level > 0 else n, 8:24, :]
            below = ocean[n + 1 if level < levels - 1 else n, 8:24, :]
            vertical = above - 2.0 * here + below
            if part == 0:
                turning = rotation * ocean[n + levels, 8:24, :]
            else:
                turning = -rotation * ocean[n - levels, 8:24, :]
            tendency = VISCOSITY * laplace + VERT_FRICTION * vertical + turning
            ocean_new[n] = wet_now * (here + DT_OCEAN * tendency)

    await_blocks(recv_sem.at[6], marks, (group - 1) * groups)
    mark = jnp.where(marks[:, 0, :] < 1, 1.0, 0.0)
    column = lax.broadcasted_iota(jnp.int32, (8, tiles), 1)
    mine = jnp.where(column == tile, 1.0, 0.0)
    mark_lanes[...] = jnp.zeros_like(mark_lanes)
    mark_lanes[:, 0:tiles] = lax.dot_general(mine, mark, (((1,), (1,)), ((), ())))

    loads[6].wait()
    loads[7].wait()
    spot8 = lax.broadcasted_iota(jnp.int32, (8, LANES), 1)
    pad_index[...] = jnp.zeros_like(pad_index)
    pad_index[0:4, :, 0:16] = o2w_index[...]
    pad_index[4:8, :, 0:16] = o2w_weight[...]
    index, weight = pad_index[0], pad_index[4]
    for k in range(1, 4):
        index = index + pltpu.roll(pad_index[k], 16 * k, 1)
        weight = weight + pltpu.roll(pad_index[4 + k], 16 * k, 1)
    index = index + pltpu.roll(index, 64, 1)
    weight = (weight + pltpu.roll(weight, 64, 1)).astype(jnp.float32)
    code, spot_index = index >> 7, index & 127
    is_east = spot8 < 64

    place_edges(edges, first, halo_w0, halo_e0)
    pltpu.make_async_copy(incoming, incoming, recv_sem.at[0]).wait()

    def pick_current(step, picked):
        for inner in range(4):
            block = step * 4 + inner
            for slot in range(2):
                a = lane_pick(jnp.broadcast_to(incoming[block, 2 * slot : 2 * slot + 1, :], (8, LANES)), spot_index)
                c = lane_pick(jnp.broadcast_to(incoming[block, 2 * slot + 1 : 2 * slot + 2, :], (8, LANES)), spot_index)
                picked = jnp.where(code == block * 2 + slot, jnp.where(is_east, a, c), picked)
        return picked

    picked = lax.fori_loop(0, tiles // 4, pick_current, jnp.zeros((8, LANES), jnp.float32))
    weighted = picked * weight
    weighted = weighted + pltpu.roll(weighted, LANES - 16, 1)
    weighted = weighted + pltpu.roll(weighted, LANES - 32, 1)
    weight = weight + pltpu.roll(weight, LANES - 16, 1)
    weight = weight + pltpu.roll(weight, LANES - 32, 1)
    currents = jnp.transpose(weighted / weight)
    for y in range(8):
        flow_x[y] = jnp.broadcast_to(currents[0:16, y : y + 1], (16, LANES))
        flow_y[y] = jnp.broadcast_to(currents[64:80, y : y + 1], (16, LANES))

    def advect(field, last):
        def one_row(y, carry):
            rows = pl.ds(pl.multiple_of(y * 16, 16), 16)
            current_x, current_y = flow_x[y], flow_y[y]
            for lo, hi in chunks(bins, LANES):
                center = field[y + 1, 8:24, lo:hi]
                flow = speed_x[0:1, lo:hi] + current_x[:, : hi - lo]
                change = flow * jnp.where(
                    flow > 0.0, center - field[y + 1, 7:23, lo:hi], field[y + 1, 9:25, lo:hi] - center
                )
                flow = speed_y[0:1, lo:hi] + current_y[:, : hi - lo]
                change += flow * jnp.where(
                    flow > 0.0, center - field[y, 8:24, lo:hi], field[y + 2, 8:24, lo:hi] - center
                )
                result = center - DT_WAVE * change
                moved[rows, lo:hi] = result
                coarse = result.astype(jnp.bfloat16)
                rounded[rows, lo:hi] = coarse
                if last:
                    leftover[rows, lo:hi] = (result - coarse.astype(jnp.float32)).astype(jnp.bfloat16)
            return carry

        lax.fori_loop(0, 8, one_row, 0)

    def react(lo, hi):
        product = jnp.dot(rounded[...], source[:, lo:hi], preferred_element_type=jnp.float32)
        return (moved[:, lo:hi] + DT_SOURCE * product).reshape(8, 16, hi - lo)

    advect(first, False)
    for lo, hi in chunks(bins, 256):
        second[1:9, 8:24, lo:hi] = react(lo, hi)
    edges2 = send_edges(11, second, edge_w1, edge_e1, halo_w1, halo_e1)
    place_edges(edges2, second, halo_w1, halo_e1)
    advect(second, True)
    sums = jnp.dot(rounded[...], mixed_t[...], preferred_element_type=jnp.float32)
    sums += jnp.dot(leftover[...], moments_t[...], preferred_element_type=jnp.float32)
    sums = jnp.transpose(sums + pltpu.roll(sums, LANES - 8, 1))
    totals[my_place * groups + my_group] = sums[0:4, :]
    spread_far(15, totals)
    parts = chunks(bins, 256)
    for lo, hi in parts[:3]:
        spectrum_new[:, :, lo:hi] = react(lo, hi)
    await_blocks(recv_sem.at[15], totals, groups - 1)
    spread_near(16, totals)
    for lo, hi in parts[3:]:
        spectrum_new[:, :, lo:hi] = react(lo, hi)
    store_spectrum = pltpu.make_async_copy(spectrum_new, spectrum_out, load_sem.at[15])
    store_spectrum.start()

    loads[13].wait()
    loads[14].wait()
    await_blocks(recv_sem.at[16], totals, (group - 1) * groups)
    marked = mark_lanes[...]
    for half in range(2):
        rows = slice(8 * half, 8 * half + 8)
        spots, codes, factors = [], [], []
        share = jnp.zeros((8, LANES), jnp.float32)
        for k in range(4):
            entry = w2o_index[k, rows, :]
            block = entry >> 7
            block = (block & (group - 1)) * groups + (block >> (group.bit_length() - 1))
            factor = w2o_weight[k, rows, :].astype(jnp.float32)
            share = share + factor
            spots.append(entry & 127)
            codes.append(block)
            factors.append(factor * lane_pick(marked, block))

        def pick_total(step, carry):
            carry = list(carry)
            for inner in range(2):
                block = step * 2 + inner
                tables = [jnp.broadcast_to(totals[block, q : q + 1, :], (8, LANES)) for q in range(4)]
                for k in range(4):
                    here = codes[k] == block
                    for q in range(4):
                        carry[4 * k + q] = jnp.where(here, lane_pick(tables[q], spots[k]), carry[4 * k + q])
            return tuple(carry)

        found = lax.fori_loop(
            0, tiles // 2, pick_total, tuple(jnp.zeros((8, LANES), jnp.float32) for _ in range(16))
        )
        forcing = []
        for q in range(4):
            total = factors[0] * found[q]
            for k in range(1, 4):
                total = total + factors[k] * found[4 * k + q]
            forcing.append(total / share)
        turn = rotation[rows]
        scale = wet_now[rows] * DT_OCEAN
        ocean_new[0, rows, :] += scale * (STRESS_COEFF * forcing[0] + turn * forcing[3])
        ocean_new[levels, rows, :] += scale * (STRESS_COEFF * forcing[1] - turn * forcing[2])
    store_ocean = pltpu.make_async_copy(ocean_new, ocean_out, load_sem.at[16])
    store_ocean.start()

    for copy in edges + ocean_edges + edges2:
        copy.wait_send()
    await_blocks(send_sem.at[0], outgoing, tiles - 1)
    for index, ref in ((5, marks), (15, totals)):
        await_blocks(send_sem.at[index], ref, groups - 1)
        await_blocks(send_sem.at[index + 1], ref, (group - 1) * groups)
    store_spectrum.wait()
    store_ocean.wait()


def on_device(
    tiles,
    bands,
    ocean_velocity,
    ocean_wet,
    coriolis,
    spectrum,
    group_speed,
    source_matrix,
    moments,
    o2w_rows,
    ocean_to_wave_index,
    o2w_weight,
    w2o_rows,
    wave_to_ocean_index,
    wave_to_ocean_weight,
):
    components, levels, rows, columns = ocean_velocity.shape
    layers = components * levels
    height, width, bins = spectrum.shape
    padded_bins = -(-bins // LANES) * LANES
    group = 1 << (max(tiles.bit_length() - 1, 2) // 2)
    angle = (np.arange(NDIR) + 0.5) * (2.0 * math.pi / NDIR)
    wheel = np.zeros((8, padded_bins), np.float32)
    wheel[0, :bins] = np.repeat(np.cos(angle), NFREQ)
    wheel[1, :bins] = np.repeat(np.sin(angle), NFREQ)
    wheel_index = np.zeros((8, padded_bins), np.int32)
    wheel_index[:, :bins] = np.tile(np.arange(NFREQ), NDIR)
    operands = (
        ocean_velocity.reshape(layers, rows, columns),
        ocean_wet,
        coriolis.reshape(1, rows),
        spectrum,
        group_speed.reshape(1, NFREQ),
        source_matrix,
        moments,
        o2w_rows[0, 0].T,
        ocean_to_wave_index,
        o2w_weight,
        w2o_rows[0, 0].T,
        wave_to_ocean_index,
        wave_to_ocean_weight,
        jnp.asarray(wheel),
        jnp.asarray(wheel_index),
    )
    f32, bf16, i32 = jnp.float32, jnp.bfloat16, jnp.int32
    V = pltpu.VMEM
    scratch = [
        V((layers, 32, columns), f32), V((rows, columns), i32), V((1, rows), f32), V((10, 32, bins), f32),
        V((1, NFREQ), f32), V((bins, bins), bf16), V((4, bins), f32),
        V((2, tiles), i32), V((4, height, width), i32), V((4, height, width), i32),
        V((4, rows, columns), i32), V((4, rows, columns), i32), V((8, padded_bins), f32), V((8, padded_bins), i32),
        V((tiles, 4, LANES), f32), V((tiles, 4, LANES), f32), V((tiles, 1, tiles), i32), V((tiles, 4, LANES), f32),
    ]
    scratch += [V((height, bins), f32)] * 8
    scratch += [V((layers, columns), f32)] * 4
    scratch += [V((8, layers * rows), f32)] * 4
    scratch += [
        V((10, 32, bins), f32), V((LANES, bins), f32), V((LANES, bins), bf16), V((LANES, bins), bf16),
        V((8, padded_bins), f32), V((8, padded_bins), f32), V((height, 16, LANES), f32), V((height, 16, LANES), f32),
        V((2, LANES, layers * rows), f32), V((8, LANES), f32), V((LANES, LANES), i32), V((8, height, LANES), i32), V((LANES, padded_bins), f32),
        V((bins, LANES), bf16), V((bins, LANES), bf16), V((8, LANES), f32),
        V((layers, rows, columns), f32), V((height, width, bins), f32),
        pltpu.SemaphoreType.DMA((17,)), pltpu.SemaphoreType.DMA((17,)), pltpu.SemaphoreType.DMA((17,)),
    ]
    any_space = pl.BlockSpec(memory_space=pl.ANY)
    ocean_next, spectrum_next = pl.pallas_call(
        functools.partial(kernel, tiles, bands, group),
        out_shape=(
            jax.ShapeDtypeStruct((layers, rows, columns), f32),
            jax.ShapeDtypeStruct((height, width, bins), f32),
        ),
        in_specs=[any_space] * len(operands),
        out_specs=(any_space, any_space),
        scratch_shapes=scratch,
        compiler_params=pltpu.CompilerParams(
            collective_id=0, has_side_effects=True, vmem_limit_bytes=48 << 20
        ),
        name="coupled_step",
    )(*operands)
    return ocean_next.reshape(ocean_velocity.shape), spectrum_next


def solution(mesh):
    placed = (
        P(None, None, "band", "tile"),
        P("band", "tile"),
        P("band"),
        P("band", "tile", None),
        P(),
        P(),
        P(),
        P("tile", "band", None, None),
        P(None, "band", "tile"),
        P(None, "band", "tile"),
        P("tile", "band", None, None),
        P(None, "band", "tile"),
        P(None, "band", "tile"),
    )
    return jax.shard_map(
        functools.partial(on_device, mesh.shape["tile"], mesh.shape["band"]),
        mesh=mesh,
        in_specs=placed,
        out_specs=(P(None, None, "band", "tile"), P("band", "tile", None)),
        check_vma=False,
    )
```

```python
import functools
import math

import jax
import jax.numpy as jnp
import numpy as np
from jax import lax
from jax.experimental import pallas as pl
from jax.experimental.pallas import tpu as pltpu
from jax.sharding import PartitionSpec as P

NDIR = 36
NFREQ = 36
DT_OCEAN = 0.2
VISCOSITY = 0.5
VERT_FRICTION = 0.5
STRESS_COEFF = 1.0
DT_WAVE = 0.1
DT_SOURCE = 0.3

LANES = 128
MESH = pl.DeviceIdType.MESH
HIGHEST = lax.Precision.HIGHEST


def chunks(total, size):
    return [(start, min(start + size, total)) for start in range(0, total, size)]


def lane_pick(table, index):
    return jnp.take_along_axis(table, index, axis=1, mode="promise_in_bounds")


def kernel(
    tiles,
    bands,
    ocean_h, wet_h, coriolis_h, spectrum_h, speed_h, source_h, moments_h,
    o2w_rows_h, o2w_index_h, o2w_weight_h, w2o_rows_h, w2o_index_h, w2o_weight_h,
    wheel_h, wheel_index_h,
    ocean_out, spectrum_out,
    ocean, wet, coriolis, first, speed, source, moments,
    o2w_rows, w2o_rows, o2w_index, o2w_weight, w2o_index, w2o_weight, wheel, wheel_index,
    outgoing, incoming, marks, totals, arrived,
    edge_w0, edge_e0, halo_w0, halo_e0, edge_w1, edge_e1, halo_w1, halo_e1,
    row_lo, row_hi, halo_lo, halo_hi, column_w, column_e, arrived_w, arrived_e,
    second, moved, rounded, leftover, speed_x, speed_y, flow_x, flow_y,
    halo_column, pad_small, pad_rows, pad_index, pad_moments, moments_t, mixed_t,
    load_sem, send_sem, recv_sem,
):
    tile, band = lax.axis_index("tile"), lax.axis_index("band")
    east, west = lax.rem(tile + 1, tiles), lax.rem(tile + tiles - 1, tiles)
    north, south = lax.rem(band + 1, bands), lax.rem(band + bands - 1, bands)
    bins = first.shape[2]
    layers = ocean.shape[0]
    levels = layers // 2

    def far_first(step):
        half = (step + 1) // 2
        return lax.rem(tile + tiles // 2 + half * (1 - 2 * (step % 2)), tiles)

    barrier = pltpu.get_barrier_semaphore()

    def greet(step, carry):
        pl.semaphore_signal(
            barrier, inc=1, device_id={"tile": far_first(step)}, device_id_type=MESH
        )
        return carry

    lax.fori_loop(0, tiles - 1, greet, 0)
    for other in (south, north):
        pl.semaphore_signal(barrier, inc=1, device_id={"band": other}, device_id_type=MESH)

    loads = [
        (ocean_h, ocean.at[:, 8:24, :]), (o2w_rows_h, o2w_rows), (spectrum_h, first.at[1:9, 8:24, :]),
        (w2o_rows_h, w2o_rows), (moments_h, moments), (source_h, source),
        (o2w_index_h, o2w_index), (o2w_weight_h, o2w_weight), (speed_h, speed), (wheel_h, wheel),
        (wheel_index_h, wheel_index), (wet_h, wet), (coriolis_h, coriolis), (w2o_index_h, w2o_index),
        (w2o_weight_h, w2o_weight),
    ]
    loads = [pltpu.make_async_copy(s, d, load_sem.at[i]) for i, (s, d) in enumerate(loads)]
    for load in loads:
        load.start()

    loads[0].wait()
    loads[1].wait()
    pad_rows[...] = jnp.zeros_like(pad_rows)
    pad_rows[0:2, 0:tiles] = o2w_rows[...]
    loads[3].wait()
    pad_rows[2:3, 0:tiles] = w2o_rows[...]
    wanted = jnp.transpose(pad_rows[...].astype(jnp.float32))
    for slot in range(2):
        row = jnp.broadcast_to(wanted[0:tiles, slot : slot + 1], (tiles, LANES))
        east_part = jnp.zeros((tiles, LANES), jnp.float32)
        north_part = east_part
        for r in range(16):
            here = row == float(r)
            east_part = jnp.where(here, ocean[0, 8 + r : 9 + r, :], east_part)
            north_part = jnp.where(here, ocean[levels, 8 + r : 9 + r, :], north_part)
        outgoing[:, 2 * slot, :] = east_part
        outgoing[:, 2 * slot + 1, :] = north_part
    marks[...] = jnp.where(jnp.broadcast_to(wanted[0:tiles, 2:3], (tiles, LANES)) < 1.0, 1.0, 0.0)

    for load in (4, 8, 9, 10):
        loads[load].wait()
    pad_small[...] = jnp.zeros_like(pad_small)
    pad_small[0:1, 0:NFREQ] = speed[...]
    speeds = jnp.broadcast_to(pad_small[0:1, :], (8, LANES))
    for lo, hi in chunks(speed_x.shape[1], LANES):
        picked = lane_pick(speeds, wheel_index[:, lo:hi])
        speed_x[:, lo:hi] = picked * wheel[0:1, lo:hi]
        speed_y[:, lo:hi] = picked * wheel[1:2, lo:hi]

    pad_moments[...] = jnp.zeros_like(pad_moments)
    pad_moments[0:4, 0:bins] = moments[...]
    for lo, hi in chunks(pad_moments.shape[1], LANES):
        top = min(hi, bins)
        part = jnp.transpose(pad_moments[:, lo:hi])
        high = part.astype(jnp.bfloat16)
        low = part - high.astype(jnp.float32)
        both = high.astype(jnp.float32) + pltpu.roll(low, 8, 1)
        moments_t[lo:top, :] = both[0 : top - lo].astype(jnp.bfloat16)
    loads[5].wait()
    lane = lax.broadcasted_iota(jnp.int32, (144, LANES), 1)

    def mix(step, carry):
        rows = pl.ds(pl.multiple_of(step * 144, 144), 144)
        mixed = jnp.dot(source[rows, :], moments_t[...], preferred_element_type=jnp.float32)
        own = moments_t[rows, :].astype(jnp.float32)
        full = own + DT_SOURCE * mixed
        full = jnp.where(lane < 8, full + pltpu.roll(full, LANES - 8, 1), 0.0)
        high = full.astype(jnp.bfloat16)
        low = full - high.astype(jnp.float32)
        both = high.astype(jnp.float32) + pltpu.roll(low, 8, 1)
        mixed_t[rows, :] = both.astype(jnp.bfloat16)
        return carry

    lax.fori_loop(0, bins // 144, mix, 0)

    pl.semaphore_wait(barrier, tiles + 1)

    keep = pltpu.make_async_copy(outgoing.at[tile], incoming.at[tile], recv_sem.at[0])
    keep.start()

    def push(index, source, target):
        def give(step, carry):
            other = far_first(step)
            pltpu.make_async_remote_copy(
                src_ref=source.at[other], dst_ref=target.at[tile], send_sem=send_sem.at[index],
                recv_sem=recv_sem.at[index], device_id={"tile": other}, device_id_type=MESH,
            ).start()
            return carry

        lax.fori_loop(0, tiles - 1, give, 0)

    push(0, outgoing, incoming)

    def send(index, src, dst, where):
        copy = pltpu.make_async_remote_copy(
            src_ref=src, dst_ref=dst, send_sem=send_sem.at[index], recv_sem=recv_sem.at[index],
            device_id=where, device_id_type=MESH,
        )
        copy.start()
        return copy

    def send_edges(base, field, edge_w, edge_e, halo_w, halo_e):
        edge_w[...] = field[1:9, 8, :]
        edge_e[...] = field[1:9, 23, :]
        return [
            send(base, field.at[1, 8:24, :], field.at[9, 8:24, :], {"band": south}),
            send(base + 1, field.at[8, 8:24, :], field.at[0, 8:24, :], {"band": north}),
            send(base + 2, edge_w, halo_e, {"tile": west}),
            send(base + 3, edge_e, halo_w, {"tile": east}),
        ]

    def place_edges(copies, field, halo_w, halo_e):
        for copy in copies:
            copy.wait_recv()
        field[1:9, 7, :] = halo_w[...] * jnp.where(tile == 0, 0.0, 1.0)
        field[1:9, 24, :] = halo_e[...] * jnp.where(tile == tiles - 1, 0.0, 1.0)

        @pl.when(band == 0)
        def _():
            field[0, 8:24, :] = jnp.zeros((16, bins), jnp.float32)

        @pl.when(band == bands - 1)
        def _():
            field[9, 8:24, :] = jnp.zeros((16, bins), jnp.float32)

    loads[2].wait()
    edges = send_edges(1, first, edge_w0, edge_e0, halo_w0, halo_e0)

    row_lo[...] = ocean[:, 8, :]
    row_hi[...] = ocean[:, 23, :]
    flat = ocean[:, 8:24, :].reshape(layers * 16, LANES)
    turned = jnp.transpose(flat)
    column_w[...] = jnp.broadcast_to(turned[0:1, :], column_w.shape)
    column_e[...] = jnp.broadcast_to(turned[LANES - 1 : LANES, :], column_e.shape)
    ocean_edges = [
        send(7, row_lo, halo_hi, {"band": south}),
        send(8, row_hi, halo_lo, {"band": north}),
    ]
    ocean_edges += [
        send(9, column_w, arrived_e, {"tile": west}),
        send(10, column_e, arrived_w, {"tile": east}),
    ]

    for copy in ocean_edges:
        copy.wait_recv()
    loads[11].wait()
    loads[12].wait()
    ocean[:, 7, :] = halo_lo[...] * jnp.where(band == 0, 0.0, 1.0)
    ocean[:, 24, :] = halo_hi[...] * jnp.where(band == bands - 1, 0.0, 1.0)
    halo_column[...] = jnp.zeros_like(halo_column)
    halo_column[0, 0:8, :] = arrived_w[...]
    halo_column[1, LANES - 8 : LANES, :] = arrived_e[...]
    column_from_w = jnp.transpose(halo_column[0]) * jnp.where(tile == 0, 0.0, 1.0)
    column_from_e = jnp.transpose(halo_column[1]) * jnp.where(tile == tiles - 1, 0.0, 1.0)
    spot = lax.broadcasted_iota(jnp.int32, (16, LANES), 1)
    line = lax.broadcasted_iota(jnp.int32, (16, LANES), 0)
    pad_small[...] = jnp.zeros_like(pad_small)
    pad_small[0:1, 0:16] = coriolis[...]
    rotation = jnp.sum(
        jnp.where(spot == line, jnp.broadcast_to(pad_small[0:1, :], (16, LANES)), 0.0),
        axis=1, keepdims=True,
    )
    rotation = jnp.broadcast_to(rotation, (16, LANES))
    wet_now = wet[...].astype(jnp.float32)
    for level in range(levels):
        for part in range(2):
            n = part * levels + level
            here = ocean[n, 8:24, :]
            lanes_w = jnp.where(spot == 0, column_from_w[16 * n : 16 * n + 16], pltpu.roll(here, 1, 1))
            lanes_e = jnp.where(
                spot == LANES - 1, column_from_e[16 * n : 16 * n + 16], pltpu.roll(here, LANES - 1, 1)
            )
            laplace = ocean[n, 7:23, :] + ocean[n, 9:25, :] + lanes_w + lanes_e - 4.0 * here
            above = ocean[n - 1 if level > 0 else n, 8:24, :]
            below = ocean[n + 1 if level < levels - 1 else n, 8:24, :]
            vertical = above - 2.0 * here + below
            if part == 0:
                turning = rotation * ocean[n + levels, 8:24, :]
            else:
                turning = -rotation * ocean[n - levels, 8:24, :]
            tendency = VISCOSITY * laplace + VERT_FRICTION * vertical + turning
            ocean_out[n] = wet_now * (here + DT_OCEAN * tendency)

    loads[6].wait()
    loads[7].wait()
    spot8 = lax.broadcasted_iota(jnp.int32, (8, LANES), 1)
    pad_index[...] = jnp.zeros_like(pad_index)
    pad_index[0:4, :, 0:16] = o2w_index[...]
    pad_index[4:8, :, 0:16] = o2w_weight[...]
    index, weight = pad_index[0], pad_index[4]
    for k in range(1, 4):
        index = index + pltpu.roll(pad_index[k], 16 * k, 1)
        weight = weight + pltpu.roll(pad_index[4 + k], 16 * k, 1)
    index = index + pltpu.roll(index, 64, 1)
    weight = (weight + pltpu.roll(weight, 64, 1)).astype(jnp.float32)
    code, spot_index = index >> 7, index & (LANES - 1)
    is_east = spot8 < 64

    place_edges(edges, first, halo_w0, halo_e0)
    pltpu.make_async_copy(incoming, incoming, recv_sem.at[0]).wait()

    def pick_current(step, picked):
        for inner in range(4):
            block = step * 4 + inner
            for slot in range(2):
                a = lane_pick(jnp.broadcast_to(incoming[block, 2 * slot : 2 * slot + 1, :], (8, LANES)), spot_index)
                c = lane_pick(jnp.broadcast_to(incoming[block, 2 * slot + 1 : 2 * slot + 2, :], (8, LANES)), spot_index)
                picked = jnp.where(code == block * 2 + slot, jnp.where(is_east, a, c), picked)
        return picked

    picked = lax.fori_loop(0, tiles // 4, pick_current, jnp.zeros((8, LANES), jnp.float32))
    weighted = picked * weight
    weighted = weighted + pltpu.roll(weighted, LANES - 16, 1)
    weighted = weighted + pltpu.roll(weighted, LANES - 32, 1)
    weight = weight + pltpu.roll(weight, LANES - 16, 1)
    weight = weight + pltpu.roll(weight, LANES - 32, 1)
    currents = jnp.transpose(weighted / weight)
    for y in range(8):
        flow_x[y] = jnp.broadcast_to(currents[0:16, y : y + 1], (16, LANES))
        flow_y[y] = jnp.broadcast_to(currents[64:80, y : y + 1], (16, LANES))

    def advect(field, last):
        def one_row(y, carry):
            rows = pl.ds(pl.multiple_of(y * 16, 16), 16)
            current_x, current_y = flow_x[y], flow_y[y]
            for lo, hi in chunks(bins, LANES):
                center = field[y + 1, 8:24, lo:hi]
                flow = speed_x[0:1, lo:hi] + current_x[:, : hi - lo]
                change = flow * jnp.where(
                    flow > 0.0, center - field[y + 1, 7:23, lo:hi], field[y + 1, 9:25, lo:hi] - center
                )
                flow = speed_y[0:1, lo:hi] + current_y[:, : hi - lo]
                change += flow * jnp.where(
                    flow > 0.0, center - field[y, 8:24, lo:hi], field[y + 2, 8:24, lo:hi] - center
                )
                result = center - DT_WAVE * change
                moved[rows, lo:hi] = result
                coarse = result.astype(jnp.bfloat16)
                rounded[rows, lo:hi] = coarse
                if last:
                    leftover[rows, lo:hi] = (result - coarse.astype(jnp.float32)).astype(jnp.bfloat16)
            return carry

        lax.fori_loop(0, 8, one_row, 0)

    def react(lo, hi):
        product = jnp.dot(rounded[...], source[:, lo:hi], preferred_element_type=jnp.float32)
        return (moved[:, lo:hi] + DT_SOURCE * product).reshape(8, 16, hi - lo)

    advect(first, False)
    for lo, hi in chunks(bins, 256):
        second[1:9, 8:24, lo:hi] = react(lo, hi)
    edges2 = send_edges(11, second, edge_w1, edge_e1, halo_w1, halo_e1)
    place_edges(edges2, second, halo_w1, halo_e1)
    advect(second, True)
    sums = jnp.dot(rounded[...], mixed_t[...], preferred_element_type=jnp.float32)
    sums += jnp.dot(leftover[...], moments_t[...], preferred_element_type=jnp.float32)
    sums = jnp.transpose(sums + pltpu.roll(sums, LANES - 8, 1))
    for q in range(4):
        totals[:, q, :] = marks[...] * sums[q : q + 1, :]
    keep_totals = pltpu.make_async_copy(totals.at[tile], arrived.at[tile], recv_sem.at[5])
    keep_totals.start()
    push(5, totals, arrived)
    for lo, hi in chunks(bins, 256):
        spectrum_out[:, :, lo:hi] = react(lo, hi)

    loads[13].wait()
    loads[14].wait()
    halves = [slice(0, 8), slice(8, 16)]
    turns = [rotation[rows] for rows in halves]
    spots, codes, factors = [], [], []
    for rows in halves:
        for k in range(4):
            entry = w2o_index[k, rows, :]
            spots.append(entry & (LANES - 1))
            codes.append(entry >> 7)
            factors.append(w2o_weight[k, rows, :].astype(jnp.float32))
    pltpu.make_async_copy(arrived, arrived, recv_sem.at[5]).wait()

    def pick_total(step, carry):
        carry = list(carry)
        for inner in range(2):
            block = step * 2 + inner
            tables = [jnp.broadcast_to(arrived[block, q : q + 1, :], (8, LANES)) for q in range(4)]
            for half in range(2):
                easts = STRESS_COEFF * tables[0] + turns[half] * tables[3]
                norths = STRESS_COEFF * tables[1] - turns[half] * tables[2]
                for k in range(4 * half, 4 * half + 4):
                    here = codes[k] == block
                    carry[k] = jnp.where(here, lane_pick(easts, spots[k]), carry[k])
                    carry[8 + k] = jnp.where(here, lane_pick(norths, spots[k]), carry[8 + k])
        return tuple(carry)

    found = lax.fori_loop(
        0, tiles // 2, pick_total, tuple(jnp.zeros((8, LANES), jnp.float32) for _ in range(16))
    )
    for half, rows in enumerate(halves):
        share, forced = factors[4 * half], [factors[4 * half] * found[4 * half + 8 * part] for part in range(2)]
        for k in range(4 * half + 1, 4 * half + 4):
            share = share + factors[k]
            forced = [forced[part] + factors[k] * found[k + 8 * part] for part in range(2)]
        scale = wet_now[rows] * DT_OCEAN
        for part in range(2):
            ocean_out[part * levels, rows, :] += scale * (forced[part] / share)

    for copy in edges + ocean_edges + edges2:
        copy.wait_send()
    for index, ref in ((0, outgoing), (5, totals)):
        sent = ref.at[pl.ds(0, tiles - 1)]
        pltpu.make_async_copy(sent, sent, send_sem.at[index]).wait()


def on_device(
    tiles,
    bands,
    ocean_velocity,
    ocean_wet,
    coriolis,
    spectrum,
    group_speed,
    source_matrix,
    moments,
    o2w_rows,
    ocean_to_wave_index,
    o2w_weight,
    w2o_rows,
    wave_to_ocean_index,
    wave_to_ocean_weight,
):
    components, levels, rows, columns = ocean_velocity.shape
    layers = components * levels
    height, width, bins = spectrum.shape
    padded_bins = -(-bins // LANES) * LANES
    angle = (np.arange(NDIR) + 0.5) * (2.0 * math.pi / NDIR)
    wheel = np.zeros((8, padded_bins), np.float32)
    wheel[0, :bins] = np.repeat(np.cos(angle), NFREQ)
    wheel[1, :bins] = np.repeat(np.sin(angle), NFREQ)
    wheel_index = np.zeros((8, padded_bins), np.int32)
    wheel_index[:, :bins] = np.tile(np.arange(NFREQ), NDIR)
    operands = (
        ocean_velocity.reshape(layers, rows, columns),
        ocean_wet,
        coriolis.reshape(1, rows),
        spectrum,
        group_speed.reshape(1, NFREQ),
        source_matrix,
        moments,
        o2w_rows[0, 0].T,
        ocean_to_wave_index,
        o2w_weight,
        w2o_rows[0, 0].T,
        wave_to_ocean_index,
        wave_to_ocean_weight,
        jnp.asarray(wheel),
        jnp.asarray(wheel_index),
    )
    f32, bf16, i32 = jnp.float32, jnp.bfloat16, jnp.int32
    V = pltpu.VMEM
    scratch = [
        V((layers, 32, columns), f32), V((rows, columns), i32), V((1, rows), f32), V((10, 32, bins), f32),
        V((1, NFREQ), f32), V((bins, bins), bf16), V((4, bins), f32),
        V((2, tiles), i32), V((1, tiles), i32), V((4, height, width), i32), V((4, height, width), i32),
        V((4, rows, columns), i32), V((4, rows, columns), i32), V((8, padded_bins), f32), V((8, padded_bins), i32),
        V((tiles, 4, LANES), f32), V((tiles, 4, LANES), f32), V((tiles, LANES), f32), V((tiles, 4, LANES), f32),
        V((tiles, 4, LANES), f32),
    ]
    scratch += [V((height, bins), f32)] * 8
    scratch += [V((layers, columns), f32)] * 4
    scratch += [V((8, layers * rows), f32)] * 4
    scratch += [
        V((10, 32, bins), f32), V((LANES, bins), f32), V((LANES, bins), bf16), V((LANES, bins), bf16),
        V((8, padded_bins), f32), V((8, padded_bins), f32), V((height, 16, LANES), f32), V((height, 16, LANES), f32),
        V((2, LANES, layers * rows), f32), V((8, LANES), f32), V((LANES, LANES), i32), V((8, height, LANES), i32), V((LANES, padded_bins), f32),
        V((bins, LANES), bf16), V((bins, LANES), bf16),
        pltpu.SemaphoreType.DMA((15,)), pltpu.SemaphoreType.DMA((15,)), pltpu.SemaphoreType.DMA((15,)),
    ]
    far_space = pl.BlockSpec(memory_space=pltpu.HBM)
    near_space = pl.BlockSpec(memory_space=pltpu.VMEM)
    ocean_next, spectrum_next = pl.pallas_call(
        functools.partial(kernel, tiles, bands),
        out_shape=(
            jax.ShapeDtypeStruct((layers, rows, columns), f32),
            jax.ShapeDtypeStruct((height, width, bins), f32),
        ),
        in_specs=[far_space] * len(operands),
        out_specs=(near_space, near_space),
        scratch_shapes=scratch,
        compiler_params=pltpu.CompilerParams(
            collective_id=0, has_side_effects=True, vmem_limit_bytes=63 << 20
        ),
        name="coupled_step",
    )(*operands)
    return ocean_next.reshape(ocean_velocity.shape), spectrum_next


def solution(mesh):
    placed = (
        P(None, None, "band", "tile"),
        P("band", "tile"),
        P("band"),
        P("band", "tile", None),
        P(),
        P(),
        P(),
        P("tile", "band", None, None),
        P(None, "band", "tile"),
        P(None, "band", "tile"),
        P("tile", "band", None, None),
        P(None, "band", "tile"),
        P(None, "band", "tile"),
    )
    return jax.shard_map(
        functools.partial(on_device, mesh.shape["tile"], mesh.shape["band"]),
        mesh=mesh,
        in_specs=placed,
        out_specs=(P(None, None, "band", "tile"), P("band", "tile", None)),
        check_vma=False,
    )
```

```python
import functools
import math

import jax
import jax.numpy as jnp
import numpy as np
from jax import lax
from jax.experimental import pallas as pl
from jax.experimental.pallas import tpu as pltpu
from jax.sharding import PartitionSpec as P

NDIR = 36
NFREQ = 36
DT_OCEAN = 0.2
VISCOSITY = 0.5
VERT_FRICTION = 0.5
STRESS_COEFF = 1.0
DT_WAVE = 0.1
DT_SOURCE = 0.3

LANES = 128
MESH = pl.DeviceIdType.MESH
HIGHEST = lax.Precision.HIGHEST


def chunks(total, size):
    return [(start, min(start + size, total)) for start in range(0, total, size)]


def lane_pick(table, index):
    return jnp.take_along_axis(table, index, axis=1, mode="promise_in_bounds")


def kernel(
    tiles,
    bands,
    ocean_h, wet_h, coriolis_h, spectrum_h, speed_h, source_h, moments_h,
    o2w_rows_h, o2w_index_h, o2w_weight_h, w2o_rows_h, w2o_index_h, w2o_weight_h,
    wheel_h, wheel_index_h,
    ocean_out, spectrum_out,
    ocean, wet, coriolis, first, speed, source, moments,
    o2w_rows, w2o_rows, o2w_index, o2w_weight, w2o_index, w2o_weight, wheel, wheel_index,
    outgoing, incoming, marks, totals, arrived,
    edge_w0, edge_e0, halo_w0, halo_e0, edge_w1, edge_e1, halo_w1, halo_e1,
    row_lo, row_hi, halo_lo, halo_hi, column_w, column_e, arrived_w, arrived_e,
    second, moved, rounded, leftover, speed_x, speed_y, flow_x, flow_y,
    halo_column, pad_small, pad_rows, pad_index, pad_moments, moments_t, mixed_t,
    load_sem, send_sem, recv_sem,
):
    tile, band = lax.axis_index("tile"), lax.axis_index("band")
    east, west = lax.rem(tile + 1, tiles), lax.rem(tile + tiles - 1, tiles)
    north, south = lax.rem(band + 1, bands), lax.rem(band + bands - 1, bands)
    bins = first.shape[2]
    layers = ocean.shape[0]
    levels = layers // 2
    unroll = min(8, tiles)

    def far_first(step):
        half = (step + 1) // 2
        return lax.rem(tile + tiles // 2 + half * (1 - 2 * (step % 2)), tiles)

    barrier = pltpu.get_barrier_semaphore()

    def greet(step, carry):
        pl.semaphore_signal(
            barrier, inc=1, device_id={"tile": far_first(step)}, device_id_type=MESH
        )
        return carry

    lax.fori_loop(0, tiles - 1, greet, 0)
    for other in (south, north):
        pl.semaphore_signal(barrier, inc=1, device_id={"band": other}, device_id_type=MESH)

    loads = [
        (ocean_h, ocean.at[:, 8:24, :]), (o2w_rows_h, o2w_rows), (spectrum_h, first.at[1:9, 8:24, :]),
        (w2o_rows_h, w2o_rows), (moments_h, moments), (source_h, source),
        (o2w_index_h, o2w_index), (o2w_weight_h, o2w_weight), (speed_h, speed), (wheel_h, wheel),
        (wheel_index_h, wheel_index), (wet_h, wet), (coriolis_h, coriolis), (w2o_index_h, w2o_index),
        (w2o_weight_h, w2o_weight),
    ]
    loads = [pltpu.make_async_copy(s, d, load_sem.at[i]) for i, (s, d) in enumerate(loads)]
    for load in loads:
        load.start()

    loads[0].wait()
    loads[1].wait()
    pad_rows[...] = jnp.zeros_like(pad_rows)
    pad_rows[0:2, 0:tiles] = o2w_rows[...]
    loads[3].wait()
    pad_rows[2:3, 0:tiles] = w2o_rows[...]
    wanted = jnp.transpose(pad_rows[...].astype(jnp.float32))
    for slot in range(2):
        row = jnp.broadcast_to(wanted[0:tiles, slot : slot + 1], (tiles, LANES))
        east_part = jnp.zeros((tiles, LANES), jnp.float32)
        north_part = east_part
        for r in range(16):
            here = row == float(r)
            east_part = jnp.where(here, ocean[0, 8 + r : 9 + r, :], east_part)
            north_part = jnp.where(here, ocean[levels, 8 + r : 9 + r, :], north_part)
        outgoing[:, 2 * slot, :] = east_part
        outgoing[:, 2 * slot + 1, :] = north_part
    marks[...] = jnp.where(jnp.broadcast_to(wanted[0:tiles, 2:3], (tiles, LANES)) < 1.0, 1.0, 0.0)

    for load in (4, 8, 9, 10):
        loads[load].wait()
    pad_small[...] = jnp.zeros_like(pad_small)
    pad_small[0:1, 0:NFREQ] = speed[...]
    speeds = jnp.broadcast_to(pad_small[0:1, :], (8, LANES))
    for lo, hi in chunks(speed_x.shape[1], LANES):
        picked = lane_pick(speeds, wheel_index[:, lo:hi])
        speed_x[:, lo:hi] = picked * wheel[0:1, lo:hi]
        speed_y[:, lo:hi] = picked * wheel[1:2, lo:hi]

    pad_moments[...] = jnp.zeros_like(pad_moments)
    pad_moments[0:4, 0:bins] = moments[...]
    for lo, hi in chunks(pad_moments.shape[1], LANES):
        top = min(hi, bins)
        part = jnp.transpose(pad_moments[:, lo:hi])
        high = part.astype(jnp.bfloat16)
        low = part - high.astype(jnp.float32)
        both = high.astype(jnp.float32) + pltpu.roll(low, 8, 1)
        moments_t[lo:top, :] = both[0 : top - lo].astype(jnp.bfloat16)
    loads[5].wait()
    lane = lax.broadcasted_iota(jnp.int32, (144, LANES), 1)

    def mix(step, carry):
        rows = pl.ds(pl.multiple_of(step * 144, 144), 144)
        mixed = jnp.dot(source[rows, :], moments_t[...], preferred_element_type=jnp.float32)
        own = moments_t[rows, :].astype(jnp.float32)
        full = own + DT_SOURCE * mixed
        full = jnp.where(lane < 8, full + pltpu.roll(full, LANES - 8, 1), 0.0)
        high = full.astype(jnp.bfloat16)
        low = full - high.astype(jnp.float32)
        both = high.astype(jnp.float32) + pltpu.roll(low, 8, 1)
        mixed_t[rows, :] = both.astype(jnp.bfloat16)
        return carry

    lax.fori_loop(0, bins // 144, mix, 0)

    pl.semaphore_wait(barrier, tiles + 1)

    keep = pltpu.make_async_copy(outgoing.at[tile], incoming.at[tile], recv_sem.at[0])
    keep.start()

    def push(index, source, target):
        def give(step, carry):
            other = far_first(step)
            pltpu.make_async_remote_copy(
                src_ref=source.at[other], dst_ref=target.at[tile], send_sem=send_sem.at[index],
                recv_sem=recv_sem.at[index], device_id={"tile": other}, device_id_type=MESH,
            ).start()
            return carry

        lax.fori_loop(0, tiles - 1, give, 0)

    push(0, outgoing, incoming)

    def send(index, src, dst, where):
        copy = pltpu.make_async_remote_copy(
            src_ref=src, dst_ref=dst, send_sem=send_sem.at[index], recv_sem=recv_sem.at[index],
            device_id=where, device_id_type=MESH,
        )
        copy.start()
        return copy

    def send_edges(base, field, edge_w, edge_e, halo_w, halo_e):
        edge_w[...] = field[1:9, 8, :]
        edge_e[...] = field[1:9, 23, :]
        return [
            send(base, field.at[1, 8:24, :], field.at[9, 8:24, :], {"band": south}),
            send(base + 1, field.at[8, 8:24, :], field.at[0, 8:24, :], {"band": north}),
            send(base + 2, edge_w, halo_e, {"tile": west}),
            send(base + 3, edge_e, halo_w, {"tile": east}),
        ]

    def place_columns(copies, field, halo_w, halo_e):
        for copy in copies[2:]:
            copy.wait_recv()
        field[1:9, 7, :] = halo_w[...] * jnp.where(tile == 0, 0.0, 1.0)
        field[1:9, 24, :] = halo_e[...] * jnp.where(tile == tiles - 1, 0.0, 1.0)

    def place_rows(copies, field):
        for copy in copies[:2]:
            copy.wait_recv()

        @pl.when(band == 0)
        def _():
            field[0, 8:24, :] = jnp.zeros((16, bins), jnp.float32)

        @pl.when(band == bands - 1)
        def _():
            field[9, 8:24, :] = jnp.zeros((16, bins), jnp.float32)

    loads[2].wait()
    edges = send_edges(1, first, edge_w0, edge_e0, halo_w0, halo_e0)

    row_lo[...] = ocean[:, 8, :]
    row_hi[...] = ocean[:, 23, :]
    flat = ocean[:, 8:24, :].reshape(layers * 16, LANES)
    turned = jnp.transpose(flat)
    column_w[...] = jnp.broadcast_to(turned[0:1, :], column_w.shape)
    column_e[...] = jnp.broadcast_to(turned[LANES - 1 : LANES, :], column_e.shape)
    ocean_edges = [
        send(7, row_lo, halo_hi, {"band": south}),
        send(8, row_hi, halo_lo, {"band": north}),
    ]
    ocean_edges += [
        send(9, column_w, arrived_e, {"tile": west}),
        send(10, column_e, arrived_w, {"tile": east}),
    ]

    for copy in ocean_edges:
        copy.wait_recv()
    loads[11].wait()
    loads[12].wait()
    ocean[:, 7, :] = halo_lo[...] * jnp.where(band == 0, 0.0, 1.0)
    ocean[:, 24, :] = halo_hi[...] * jnp.where(band == bands - 1, 0.0, 1.0)
    halo_column[...] = jnp.zeros_like(halo_column)
    halo_column[0, 0:8, :] = arrived_w[...]
    halo_column[1, LANES - 8 : LANES, :] = arrived_e[...]
    column_from_w = jnp.transpose(halo_column[0]) * jnp.where(tile == 0, 0.0, 1.0)
    column_from_e = jnp.transpose(halo_column[1]) * jnp.where(tile == tiles - 1, 0.0, 1.0)
    spot = lax.broadcasted_iota(jnp.int32, (16, LANES), 1)
    line = lax.broadcasted_iota(jnp.int32, (16, LANES), 0)
    pad_small[...] = jnp.zeros_like(pad_small)
    pad_small[0:1, 0:16] = coriolis[...]
    rotation = jnp.sum(
        jnp.where(spot == line, jnp.broadcast_to(pad_small[0:1, :], (16, LANES)), 0.0),
        axis=1, keepdims=True,
    )
    rotation = jnp.broadcast_to(rotation, (16, LANES))
    wet_now = wet[...].astype(jnp.float32)
    for level in range(levels):
        for part in range(2):
            n = part * levels + level
            here = ocean[n, 8:24, :]
            lanes_w = jnp.where(spot == 0, column_from_w[16 * n : 16 * n + 16], pltpu.roll(here, 1, 1))
            lanes_e = jnp.where(
                spot == LANES - 1, column_from_e[16 * n : 16 * n + 16], pltpu.roll(here, LANES - 1, 1)
            )
            laplace = ocean[n, 7:23, :] + ocean[n, 9:25, :] + lanes_w + lanes_e - 4.0 * here
            above = ocean[n - 1 if level > 0 else n, 8:24, :]
            below = ocean[n + 1 if level < levels - 1 else n, 8:24, :]
            vertical = above - 2.0 * here + below
            if part == 0:
                turning = rotation * ocean[n + levels, 8:24, :]
            else:
                turning = -rotation * ocean[n - levels, 8:24, :]
            tendency = VISCOSITY * laplace + VERT_FRICTION * vertical + turning
            ocean_out[n] = wet_now * (here + DT_OCEAN * tendency)

    loads[6].wait()
    loads[7].wait()
    spot8 = lax.broadcasted_iota(jnp.int32, (8, LANES), 1)
    pad_index[...] = jnp.zeros_like(pad_index)
    pad_index[0:4, :, 0:16] = o2w_index[...]
    pad_index[4:8, :, 0:16] = o2w_weight[...]
    index, weight = pad_index[0], pad_index[4]
    for k in range(1, 4):
        index = index + pltpu.roll(pad_index[k], 16 * k, 1)
        weight = weight + pltpu.roll(pad_index[4 + k], 16 * k, 1)
    index = index + pltpu.roll(index, 64, 1)
    weight = (weight + pltpu.roll(weight, 64, 1)).astype(jnp.float32)
    code, spot_index = index >> 7, index & (LANES - 1)
    is_east = spot8 < 64

    place_columns(edges, first, halo_w0, halo_e0)
    place_rows(edges, first)
    pltpu.make_async_copy(incoming, incoming, recv_sem.at[0]).wait()

    def pick_current(step, picked):
        for inner in range(unroll):
            block = step * unroll + inner
            for slot in range(2):
                a = lane_pick(jnp.broadcast_to(incoming[block, 2 * slot : 2 * slot + 1, :], (8, LANES)), spot_index)
                c = lane_pick(jnp.broadcast_to(incoming[block, 2 * slot + 1 : 2 * slot + 2, :], (8, LANES)), spot_index)
                picked = jnp.where(code == block * 2 + slot, jnp.where(is_east, a, c), picked)
        return picked

    picked = lax.fori_loop(0, tiles // unroll, pick_current, jnp.zeros((8, LANES), jnp.float32))
    weighted = picked * weight
    weighted = weighted + pltpu.roll(weighted, LANES - 16, 1)
    weighted = weighted + pltpu.roll(weighted, LANES - 32, 1)
    weight = weight + pltpu.roll(weight, LANES - 16, 1)
    weight = weight + pltpu.roll(weight, LANES - 32, 1)
    currents = jnp.transpose(weighted / weight)
    for y in range(8):
        flow_x[y] = jnp.broadcast_to(currents[0:16, y : y + 1], (16, LANES))
        flow_y[y] = jnp.broadcast_to(currents[64:80, y : y + 1], (16, LANES))

    def advect(field, last, row_of, count):
        def one_row(step, carry):
            y = row_of(step)
            rows = pl.ds(pl.multiple_of(y * 16, 16), 16)
            current_x, current_y = flow_x[y], flow_y[y]
            for lo, hi in chunks(bins, LANES):
                center = field[y + 1, 8:24, lo:hi]
                flow = speed_x[0:1, lo:hi] + current_x[:, : hi - lo]
                change = flow * jnp.where(
                    flow > 0.0, center - field[y + 1, 7:23, lo:hi], field[y + 1, 9:25, lo:hi] - center
                )
                flow = speed_y[0:1, lo:hi] + current_y[:, : hi - lo]
                change += flow * jnp.where(
                    flow > 0.0, center - field[y, 8:24, lo:hi], field[y + 2, 8:24, lo:hi] - center
                )
                result = center - DT_WAVE * change
                moved[rows, lo:hi] = result
                coarse = result.astype(jnp.bfloat16)
                rounded[rows, lo:hi] = coarse
                if last:
                    leftover[rows, lo:hi] = (result - coarse.astype(jnp.float32)).astype(jnp.bfloat16)
            return carry

        lax.fori_loop(0, count, one_row, 0)

    def react(lo, hi):
        product = jnp.dot(rounded[...], source[:, lo:hi], preferred_element_type=jnp.float32)
        return (moved[:, lo:hi] + DT_SOURCE * product).reshape(8, 16, hi - lo)

    advect(first, False, lambda step: step, 8)
    for lo, hi in chunks(bins, 256):
        second[1:9, 8:24, lo:hi] = react(lo, hi)
    edges2 = send_edges(11, second, edge_w1, edge_e1, halo_w1, halo_e1)
    place_columns(edges2, second, halo_w1, halo_e1)
    advect(second, True, lambda step: step + 1, 6)
    place_rows(edges2, second)
    advect(second, True, lambda step: step * 7, 2)
    sums = jnp.dot(rounded[...], mixed_t[...], preferred_element_type=jnp.float32)
    sums += jnp.dot(leftover[...], moments_t[...], preferred_element_type=jnp.float32)
    sums = jnp.transpose(sums + pltpu.roll(sums, LANES - 8, 1))
    for q in range(4):
        totals[:, q, :] = marks[...] * sums[q : q + 1, :]
    keep_totals = pltpu.make_async_copy(totals.at[tile], arrived.at[tile], recv_sem.at[5])
    keep_totals.start()
    push(5, totals, arrived)
    for lo, hi in chunks(bins, 256):
        spectrum_out[:, :, lo:hi] = react(lo, hi)

    loads[13].wait()
    loads[14].wait()
    halves = [slice(0, 8), slice(8, 16)]
    turns = [rotation[rows] for rows in halves]
    spots, codes, factors = [], [], []
    for rows in halves:
        for k in range(4):
            entry = w2o_index[k, rows, :]
            spots.append(entry & (LANES - 1))
            codes.append(entry >> 7)
            factors.append(w2o_weight[k, rows, :].astype(jnp.float32))
    pltpu.make_async_copy(arrived, arrived, recv_sem.at[5]).wait()

    def pick_total(step, carry):
        carry = list(carry)
        for inner in range(unroll):
            block = step * unroll + inner
            tables = [jnp.broadcast_to(arrived[block, q : q + 1, :], (8, LANES)) for q in range(4)]
            for half in range(2):
                easts = STRESS_COEFF * tables[0] + turns[half] * tables[3]
                norths = STRESS_COEFF * tables[1] - turns[half] * tables[2]
                for k in range(4 * half, 4 * half + 4):
                    here = codes[k] == block
                    carry[k] = jnp.where(here, lane_pick(easts, spots[k]), carry[k])
                    carry[8 + k] = jnp.where(here, lane_pick(norths, spots[k]), carry[8 + k])
        return tuple(carry)

    found = lax.fori_loop(
        0, tiles // unroll, pick_total, tuple(jnp.zeros((8, LANES), jnp.float32) for _ in range(16))
    )
    for half, rows in enumerate(halves):
        share, forced = factors[4 * half], [factors[4 * half] * found[4 * half + 8 * part] for part in range(2)]
        for k in range(4 * half + 1, 4 * half + 4):
            share = share + factors[k]
            forced = [forced[part] + factors[k] * found[k + 8 * part] for part in range(2)]
        scale = wet_now[rows] * DT_OCEAN
        for part in range(2):
            ocean_out[part * levels, rows, :] += scale * (forced[part] / share)

    for copy in edges + ocean_edges + edges2:
        copy.wait_send()
    for index, ref in ((0, outgoing), (5, totals)):
        sent = ref.at[pl.ds(0, tiles - 1)]
        pltpu.make_async_copy(sent, sent, send_sem.at[index]).wait()


def on_device(
    tiles,
    bands,
    ocean_velocity,
    ocean_wet,
    coriolis,
    spectrum,
    group_speed,
    source_matrix,
    moments,
    o2w_rows,
    ocean_to_wave_index,
    o2w_weight,
    w2o_rows,
    wave_to_ocean_index,
    wave_to_ocean_weight,
):
    components, levels, rows, columns = ocean_velocity.shape
    layers = components * levels
    height, width, bins = spectrum.shape
    padded_bins = -(-bins // LANES) * LANES
    angle = (np.arange(NDIR) + 0.5) * (2.0 * math.pi / NDIR)
    wheel = np.zeros((8, padded_bins), np.float32)
    wheel[0, :bins] = np.repeat(np.cos(angle), NFREQ)
    wheel[1, :bins] = np.repeat(np.sin(angle), NFREQ)
    wheel_index = np.zeros((8, padded_bins), np.int32)
    wheel_index[:, :bins] = np.tile(np.arange(NFREQ), NDIR)
    operands = (
        ocean_velocity.reshape(layers, rows, columns),
        ocean_wet,
        coriolis.reshape(1, rows),
        spectrum,
        group_speed.reshape(1, NFREQ),
        source_matrix,
        moments,
        o2w_rows[0, 0].T,
        ocean_to_wave_index,
        o2w_weight,
        w2o_rows[0, 0].T,
        wave_to_ocean_index,
        wave_to_ocean_weight,
        jnp.asarray(wheel),
        jnp.asarray(wheel_index),
    )
    f32, bf16, i32 = jnp.float32, jnp.bfloat16, jnp.int32
    V = pltpu.VMEM
    scratch = [
        V((layers, 32, columns), f32), V((rows, columns), i32), V((1, rows), f32), V((10, 32, bins), f32),
        V((1, NFREQ), f32), V((bins, bins), bf16), V((4, bins), f32),
        V((2, tiles), i32), V((1, tiles), i32), V((4, height, width), i32), V((4, height, width), i32),
        V((4, rows, columns), i32), V((4, rows, columns), i32), V((8, padded_bins), f32), V((8, padded_bins), i32),
        V((tiles, 4, LANES), f32), V((tiles, 4, LANES), f32), V((tiles, LANES), f32), V((tiles, 4, LANES), f32),
        V((tiles, 4, LANES), f32),
    ]
    scratch += [V((height, bins), f32)] * 8
    scratch += [V((layers, columns), f32)] * 4
    scratch += [V((8, layers * rows), f32)] * 4
    scratch += [
        V((10, 32, bins), f32), V((LANES, bins), f32), V((LANES, bins), bf16), V((LANES, bins), bf16),
        V((8, padded_bins), f32), V((8, padded_bins), f32), V((height, 16, LANES), f32), V((height, 16, LANES), f32),
        V((2, LANES, layers * rows), f32), V((8, LANES), f32), V((LANES, LANES), i32), V((8, height, LANES), i32), V((LANES, padded_bins), f32),
        V((bins, LANES), bf16), V((bins, LANES), bf16),
        pltpu.SemaphoreType.DMA((15,)), pltpu.SemaphoreType.DMA((15,)), pltpu.SemaphoreType.DMA((15,)),
    ]
    far_space = pl.BlockSpec(memory_space=pltpu.HBM)
    near_space = pl.BlockSpec(memory_space=pltpu.VMEM)
    ocean_next, spectrum_next = pl.pallas_call(
        functools.partial(kernel, tiles, bands),
        out_shape=(
            pltpu.VMEM((layers, rows, columns), f32),
            pltpu.VMEM((height, width, bins), f32),
        ),
        in_specs=[far_space] * len(operands),
        out_specs=(near_space, near_space),
        scratch_shapes=scratch,
        compiler_params=pltpu.CompilerParams(
            collective_id=0, has_side_effects=True, vmem_limit_bytes=60 << 20
        ),
        name="coupled_step",
    )(*operands)
    return ocean_next.reshape(ocean_velocity.shape), spectrum_next


def solution(mesh):
    placed = (
        P(None, None, "band", "tile"),
        P("band", "tile"),
        P("band"),
        P("band", "tile", None),
        P(),
        P(),
        P(),
        P("tile", "band", None, None),
        P(None, "band", "tile"),
        P(None, "band", "tile"),
        P("tile", "band", None, None),
        P(None, "band", "tile"),
        P(None, "band", "tile"),
    )
    return jax.shard_map(
        functools.partial(on_device, mesh.shape["tile"], mesh.shape["band"]),
        mesh=mesh,
        in_specs=placed,
        out_specs=(P(None, None, "band", "tile"), P("band", "tile", None)),
        check_vma=False,
    )
```

```python
import functools
import math

import jax
import jax.numpy as jnp
import numpy as np
from jax import lax
from jax.experimental import pallas as pl
from jax.experimental.pallas import tpu as pltpu
from jax.sharding import PartitionSpec as P

NDIR = 36
NFREQ = 36
DT_OCEAN = 0.2
VISCOSITY = 0.5
VERT_FRICTION = 0.5
STRESS_COEFF = 1.0
DT_WAVE = 0.1
DT_SOURCE = 0.3

LANES = 128
MESH = pl.DeviceIdType.MESH
HIGHEST = lax.Precision.HIGHEST


def chunks(total, size):
    return [(start, min(start + size, total)) for start in range(0, total, size)]


def lane_pick(table, index):
    return jnp.take_along_axis(table, index, axis=1, mode="promise_in_bounds")


def kernel(
    tiles,
    bands,
    ocean_h, wet_h, coriolis_h, spectrum_h, speed_h, source_h, moments_h,
    o2w_rows_h, o2w_index_h, o2w_weight_h, w2o_rows_h, w2o_index_h, w2o_weight_h,
    wheel_h, wheel_index_h,
    ocean_out, spectrum_out,
    ocean, wet, coriolis, first, speed, source, moments,
    o2w_rows, o2w_index, o2w_weight, w2o_index, w2o_weight, wheel, wheel_index,
    outgoing, incoming, marks, arrived,
    edge_w0, edge_e0, halo_w0, halo_e0, edge_w1, edge_e1, halo_w1, halo_e1,
    row_lo, row_hi, halo_lo, halo_hi, column_w, column_e, arrived_w, arrived_e,
    second, steps, moved, rounded, leftover, speed_x, speed_y, flow_x, flow_y,
    halo_column, pad_small, pad_rows, pad_index, pad_moments, moments_t, mixed_t,
    load_sem, send_sem, recv_sem,
):
    tile, band = lax.axis_index("tile"), lax.axis_index("band")
    east, west = lax.rem(tile + 1, tiles), lax.rem(tile + tiles - 1, tiles)
    north, south = lax.rem(band + 1, bands), lax.rem(band + bands - 1, bands)
    bins = first.shape[2]
    layers = ocean.shape[0]
    levels = layers // 2
    unroll = min(8, tiles // 2)
    half_tiles = tiles // 2
    chip, core = tile // 2, tile % 2
    own = core * half_tiles + chip
    same_core = pl.ds(core * half_tiles, half_tiles)

    def far_first(step):
        half = (step + 1) // 2
        return lax.rem(tile + tiles // 2 + half * (1 - 2 * (step % 2)), tiles)

    barrier = pltpu.get_barrier_semaphore()

    def greet(step, carry):
        pl.semaphore_signal(
            barrier, inc=1, device_id={"tile": far_first(step)}, device_id_type=MESH
        )
        return carry

    lax.fori_loop(0, tiles - 1, greet, 0)
    for other in (south, north):
        pl.semaphore_signal(barrier, inc=1, device_id={"band": other}, device_id_type=MESH)

    loads = [
        (ocean_h, ocean.at[:, 8:24, :]), (o2w_rows_h, o2w_rows), (spectrum_h, first.at[1:9, 8:24, :]),
        (w2o_rows_h, marks.at[own]), (moments_h, moments), (source_h, source),
        (o2w_index_h, o2w_index), (o2w_weight_h, o2w_weight), (speed_h, speed), (wheel_h, wheel),
        (wheel_index_h, wheel_index), (wet_h, wet), (coriolis_h, coriolis), (w2o_index_h, w2o_index),
        (w2o_weight_h, w2o_weight),
    ]
    loads = [pltpu.make_async_copy(s, d, load_sem.at[i]) for i, (s, d) in enumerate(loads)]
    for load in loads:
        load.start()

    loads[0].wait()
    loads[1].wait()
    pad_rows[...] = jnp.zeros_like(pad_rows)
    pad_rows[0:2, 0:tiles] = o2w_rows[...]
    wanted = jnp.transpose(pad_rows[...].astype(jnp.float32))
    for slot in range(2):
        row = jnp.broadcast_to(wanted[0:tiles, slot : slot + 1], (tiles, LANES))
        east_part = jnp.zeros((tiles, LANES), jnp.float32)
        north_part = east_part
        for r in range(16):
            here = row == float(r)
            east_part = jnp.where(here, ocean[0, 8 + r : 9 + r, :], east_part)
            north_part = jnp.where(here, ocean[levels, 8 + r : 9 + r, :], north_part)
        outgoing[:, 2 * slot, :] = east_part
        outgoing[:, 2 * slot + 1, :] = north_part

    for load in (4, 8, 9, 10):
        loads[load].wait()
    pad_small[...] = jnp.zeros_like(pad_small)
    pad_small[0:1, 0:NFREQ] = speed[...]
    speeds = jnp.broadcast_to(pad_small[0:1, :], (8, LANES))
    for lo, hi in chunks(speed_x.shape[1], LANES):
        picked = lane_pick(speeds, wheel_index[:, lo:hi])
        speed_x[:, lo:hi] = picked * wheel[0:1, lo:hi]
        speed_y[:, lo:hi] = picked * wheel[1:2, lo:hi]

    pad_moments[...] = jnp.zeros_like(pad_moments)
    pad_moments[0:4, 0:bins] = moments[...]
    for lo, hi in chunks(pad_moments.shape[1], LANES):
        top = min(hi, bins)
        part = jnp.transpose(pad_moments[:, lo:hi])
        high = part.astype(jnp.bfloat16)
        low = part - high.astype(jnp.float32)
        both = high.astype(jnp.float32) + pltpu.roll(low, 8, 1)
        moments_t[lo:top, :] = both[0 : top - lo].astype(jnp.bfloat16)
    loads[5].wait()
    lane = lax.broadcasted_iota(jnp.int32, (144, LANES), 1)

    def mix(step, carry):
        rows = pl.ds(pl.multiple_of(step * 144, 144), 144)
        mixed = jnp.dot(source[rows, :], moments_t[...], preferred_element_type=jnp.float32)
        own = moments_t[rows, :].astype(jnp.float32)
        full = own + DT_SOURCE * mixed
        full = jnp.where(lane < 8, full + pltpu.roll(full, LANES - 8, 1), 0.0)
        high = full.astype(jnp.bfloat16)
        low = full - high.astype(jnp.float32)
        both = high.astype(jnp.float32) + pltpu.roll(low, 8, 1)
        mixed_t[rows, :] = both.astype(jnp.bfloat16)
        return carry

    lax.fori_loop(0, bins // 144, mix, 0)

    pl.semaphore_wait(barrier, tiles + 1)

    keep = pltpu.make_async_copy(outgoing.at[tile], incoming.at[tile], recv_sem.at[0])
    keep.start()

    def give_rows(step, carry):
        other = far_first(step)
        pltpu.make_async_remote_copy(
            src_ref=outgoing.at[other], dst_ref=incoming.at[tile], send_sem=send_sem.at[0],
            recv_sem=recv_sem.at[0], device_id={"tile": other}, device_id_type=MESH,
        ).start()
        return carry

    lax.fori_loop(0, tiles - 1, give_rows, 0)

    def send(index, src, dst, where):
        copy = pltpu.make_async_remote_copy(
            src_ref=src, dst_ref=dst, send_sem=send_sem.at[index], recv_sem=recv_sem.at[index],
            device_id=where, device_id_type=MESH,
        )
        copy.start()
        return copy

    def spread(index, ref):
        def give(step, carry):
            other = half_tiles // 2 + (step + 1) // 2 * (1 - 2 * (step % 2))
            other = 2 * lax.rem(chip + other, half_tiles) + core
            pltpu.make_async_remote_copy(
                src_ref=ref.at[own], dst_ref=ref.at[own], send_sem=send_sem.at[index],
                recv_sem=recv_sem.at[index], device_id={"tile": other}, device_id_type=MESH,
            ).start()
            return carry

        lax.fori_loop(0, half_tiles - 1, give, 0)

    def pass_on(index, ref):
        part = ref.at[pl.ds(0, half_tiles - 1)]
        pltpu.make_async_copy(part, part, recv_sem.at[index]).wait()
        return send(index + 1, ref.at[same_core], ref.at[same_core], {"tile": tile + 1 - 2 * core})

    def send_edges(base, field, edge_w, edge_e, halo_w, halo_e, lanes):
        edge_w[:, lanes] = field[1:9, 8, lanes]
        edge_e[:, lanes] = field[1:9, 23, lanes]
        return [
            send(base, field.at[1, 8:24, lanes], field.at[9, 8:24, lanes], {"band": south}),
            send(base + 1, field.at[8, 8:24, lanes], field.at[0, 8:24, lanes], {"band": north}),
            send(base + 2, edge_w.at[:, lanes], halo_e.at[:, lanes], {"tile": west}),
            send(base + 3, edge_e.at[:, lanes], halo_w.at[:, lanes], {"tile": east}),
        ]

    def place_columns(copies, field, halo_w, halo_e):
        for copy in copies[2::4] + copies[3::4]:
            copy.wait_recv()
        field[1:9, 7, :] = halo_w[...] * jnp.where(tile == 0, 0.0, 1.0)
        field[1:9, 24, :] = halo_e[...] * jnp.where(tile == tiles - 1, 0.0, 1.0)

    def place_rows(copies, field):
        for copy in copies[0::4] + copies[1::4]:
            copy.wait_recv()

        @pl.when(band == 0)
        def _():
            field[0, 8:24, :] = jnp.zeros((16, bins), jnp.float32)

        @pl.when(band == bands - 1)
        def _():
            field[9, 8:24, :] = jnp.zeros((16, bins), jnp.float32)

    loads[2].wait()
    edges = send_edges(15, first, edge_w0, edge_e0, halo_w0, halo_e0, slice(0, bins))

    loads[3].wait()
    spread(1, marks)
    row_lo[...] = ocean[:, 8, :]
    row_hi[...] = ocean[:, 23, :]
    flat = ocean[:, 8:24, :].reshape(layers * 16, LANES)
    turned = jnp.transpose(flat)
    column_w[...] = jnp.broadcast_to(turned[0:1, :], column_w.shape)
    column_e[...] = jnp.broadcast_to(turned[LANES - 1 : LANES, :], column_e.shape)
    ocean_edges = [
        send(7, row_lo, halo_hi, {"band": south}),
        send(8, row_hi, halo_lo, {"band": north}),
    ]
    ocean_edges += [
        send(9, column_w, arrived_e, {"tile": west}),
        send(10, column_e, arrived_w, {"tile": east}),
    ]

    for copy in ocean_edges:
        copy.wait_recv()
    loads[11].wait()
    loads[12].wait()
    ocean[:, 7, :] = halo_lo[...] * jnp.where(band == 0, 0.0, 1.0)
    ocean[:, 24, :] = halo_hi[...] * jnp.where(band == bands - 1, 0.0, 1.0)
    halo_column[...] = jnp.zeros_like(halo_column)
    halo_column[0, 0:8, :] = arrived_w[...]
    halo_column[1, LANES - 8 : LANES, :] = arrived_e[...]
    column_from_w = jnp.transpose(halo_column[0]) * jnp.where(tile == 0, 0.0, 1.0)
    column_from_e = jnp.transpose(halo_column[1]) * jnp.where(tile == tiles - 1, 0.0, 1.0)
    spot = lax.broadcasted_iota(jnp.int32, (16, LANES), 1)
    line = lax.broadcasted_iota(jnp.int32, (16, LANES), 0)
    pad_small[...] = jnp.zeros_like(pad_small)
    pad_small[0:1, 0:16] = coriolis[...]
    rotation = jnp.sum(
        jnp.where(spot == line, jnp.broadcast_to(pad_small[0:1, :], (16, LANES)), 0.0),
        axis=1, keepdims=True,
    )
    rotation = jnp.broadcast_to(rotation, (16, LANES))
    wet_now = wet[...].astype(jnp.float32)
    for level in range(levels):
        for part in range(2):
            n = part * levels + level
            here = ocean[n, 8:24, :]
            lanes_w = jnp.where(spot == 0, column_from_w[16 * n : 16 * n + 16], pltpu.roll(here, 1, 1))
            lanes_e = jnp.where(
                spot == LANES - 1, column_from_e[16 * n : 16 * n + 16], pltpu.roll(here, LANES - 1, 1)
            )
            laplace = ocean[n, 7:23, :] + ocean[n, 9:25, :] + lanes_w + lanes_e - 4.0 * here
            above = ocean[n - 1 if level > 0 else n, 8:24, :]
            below = ocean[n + 1 if level < levels - 1 else n, 8:24, :]
            vertical = above - 2.0 * here + below
            if part == 0:
                turning = rotation * ocean[n + levels, 8:24, :]
            else:
                turning = -rotation * ocean[n - levels, 8:24, :]
            tendency = VISCOSITY * laplace + VERT_FRICTION * vertical + turning
            ocean_out[n] = wet_now * (here + DT_OCEAN * tendency)

    loads[6].wait()
    loads[7].wait()
    spot8 = lax.broadcasted_iota(jnp.int32, (8, LANES), 1)
    pad_index[...] = jnp.zeros_like(pad_index)
    pad_index[0:4, :, 0:16] = o2w_index[...]
    pad_index[4:8, :, 0:16] = o2w_weight[...]
    index, weight = pad_index[0], pad_index[4]
    for k in range(1, 4):
        index = index + pltpu.roll(pad_index[k], 16 * k, 1)
        weight = weight + pltpu.roll(pad_index[4 + k], 16 * k, 1)
    index = index + pltpu.roll(index, 64, 1)
    weight = (weight + pltpu.roll(weight, 64, 1)).astype(jnp.float32)
    code, spot_index = index >> 7, index & (LANES - 1)
    is_east = spot8 < 64

    place_columns(edges, first, halo_w0, halo_e0)
    place_rows(edges, first)

    def differences(y, carry):
        for lo, hi in chunks(bins, LANES):
            center = first[y + 1, 8:24, lo:hi]
            steps[0, y, :, lo:hi] = center - first[y + 1, 7:23, lo:hi]
            steps[1, y, :, lo:hi] = first[y + 1, 9:25, lo:hi] - center
            steps[2, y, :, lo:hi] = center - first[y, 8:24, lo:hi]
            steps[3, y, :, lo:hi] = first[y + 2, 8:24, lo:hi] - center
        return carry

    lax.fori_loop(0, 8, differences, 0)

    def pick_current(block, picked):
        for slot in range(2):
            a = lane_pick(jnp.broadcast_to(incoming[block, 2 * slot : 2 * slot + 1, :], (8, LANES)), spot_index)
            c = lane_pick(jnp.broadcast_to(incoming[block, 2 * slot + 1 : 2 * slot + 2, :], (8, LANES)), spot_index)
            picked = jnp.where(code == block * 2 + slot, jnp.where(is_east, a, c), picked)
        return picked

    def several_currents(step, picked):
        for inner in range(unroll):
            picked = pick_current(step * unroll + inner, picked)
        return picked

    pltpu.make_async_copy(incoming, incoming, recv_sem.at[0]).wait()
    picked = lax.fori_loop(0, tiles // unroll, several_currents, jnp.zeros((8, LANES), jnp.float32))
    weighted = picked * weight
    weighted = weighted + pltpu.roll(weighted, LANES - 16, 1)
    weighted = weighted + pltpu.roll(weighted, LANES - 32, 1)
    weight = weight + pltpu.roll(weight, LANES - 16, 1)
    weight = weight + pltpu.roll(weight, LANES - 32, 1)
    currents = jnp.transpose(weighted / weight)
    for y in range(8):
        flow_x[y] = jnp.broadcast_to(currents[0:16, y : y + 1], (16, LANES))
        flow_y[y] = jnp.broadcast_to(currents[64:80, y : y + 1], (16, LANES))

    def settle(rows, lo, hi, center, change, last):
        result = center - DT_WAVE * change
        moved[rows, lo:hi] = result
        coarse = result.astype(jnp.bfloat16)
        rounded[rows, lo:hi] = coarse
        if last:
            leftover[rows, lo:hi] = (result - coarse.astype(jnp.float32)).astype(jnp.bfloat16)

    def advect_first(y, carry):
        rows = pl.ds(pl.multiple_of(y * 16, 16), 16)
        current_x, current_y = flow_x[y], flow_y[y]
        for lo, hi in chunks(bins, LANES):
            flow = speed_x[0:1, lo:hi] + current_x[:, : hi - lo]
            change = flow * jnp.where(flow > 0.0, steps[0, y, :, lo:hi], steps[1, y, :, lo:hi])
            flow = speed_y[0:1, lo:hi] + current_y[:, : hi - lo]
            change += flow * jnp.where(flow > 0.0, steps[2, y, :, lo:hi], steps[3, y, :, lo:hi])
            settle(rows, lo, hi, first[y + 1, 8:24, lo:hi], change, False)
        return carry

    def advect(field, row_of, count):
        def one_row(step, carry):
            y = row_of(step)
            rows = pl.ds(pl.multiple_of(y * 16, 16), 16)
            current_x, current_y = flow_x[y], flow_y[y]
            for lo, hi in chunks(bins, LANES):
                center = field[y + 1, 8:24, lo:hi]
                flow = speed_x[0:1, lo:hi] + current_x[:, : hi - lo]
                change = flow * jnp.where(
                    flow > 0.0, center - field[y + 1, 7:23, lo:hi], field[y + 1, 9:25, lo:hi] - center
                )
                flow = speed_y[0:1, lo:hi] + current_y[:, : hi - lo]
                change += flow * jnp.where(
                    flow > 0.0, center - field[y, 8:24, lo:hi], field[y + 2, 8:24, lo:hi] - center
                )
                settle(rows, lo, hi, center, change, True)
            return carry

        lax.fori_loop(0, count, one_row, 0)

    def react(lo, hi):
        product = jnp.dot(rounded[...], source[:, lo:hi], preferred_element_type=jnp.float32)
        return (moved[:, lo:hi] + DT_SOURCE * product).reshape(8, 16, hi - lo)

    lax.fori_loop(0, 8, advect_first, 0)
    for lo, hi in chunks(bins, 256):
        second[1:9, 8:24, lo:hi] = react(lo, hi)
    edges2 = send_edges(11, second, edge_w1, edge_e1, halo_w1, halo_e1, slice(0, bins))
    passed_marks = pass_on(1, marks)
    place_columns(edges2, second, halo_w1, halo_e1)
    advect(second, lambda step: step + 1, 6)
    place_rows(edges2, second)
    advect(second, lambda step: step * 7, 2)
    sums = jnp.dot(rounded[...], mixed_t[...], preferred_element_type=jnp.float32)
    sums += jnp.dot(leftover[...], moments_t[...], preferred_element_type=jnp.float32)
    sums = jnp.transpose(sums + pltpu.roll(sums, LANES - 8, 1))
    arrived[own] = sums[0:4, :]
    spread(5, arrived)
    for lo, hi in chunks(bins, 256):
        spectrum_out[:, :, lo:hi] = react(lo, hi)

    loads[13].wait()
    loads[14].wait()
    halves = [slice(0, 8), slice(8, 16)]
    turns = [rotation[rows] for rows in halves]
    passed_marks.wait_recv()
    mine = jnp.where(lax.broadcasted_iota(jnp.int32, (8, tiles), 1) == tile, 1.0, 0.0)
    mark = jnp.where(marks[:, 0, :] < 1, 1.0, 0.0)
    pad_small[...] = jnp.zeros_like(pad_small)
    pad_small[:, 0:tiles] = lax.dot_general(mine, mark, (((1,), (1,)), ((), ())))
    marked = pad_small[...]
    spots, codes, factors, shares = [], [], [], []
    for rows in halves:
        for k in range(4):
            entry = w2o_index[k, rows, :]
            spots.append(entry & (LANES - 1))
            block = entry >> 7
            block = (block & 1) * half_tiles + (block >> 1)
            codes.append(block)
            factor = w2o_weight[k, rows, :].astype(jnp.float32)
            shares.append(factor)
            factors.append(factor * lane_pick(marked, block))

    def pick_total(block, carry):
        carry = list(carry)
        tables = [jnp.broadcast_to(arrived[block, q : q + 1, :], (8, LANES)) for q in range(4)]
        for half in range(2):
            easts = STRESS_COEFF * tables[0] + turns[half] * tables[3]
            norths = STRESS_COEFF * tables[1] - turns[half] * tables[2]
            for k in range(4 * half, 4 * half + 4):
                here = codes[k] == block
                carry[k] = jnp.where(here, lane_pick(easts, spots[k]), carry[k])
                carry[8 + k] = jnp.where(here, lane_pick(norths, spots[k]), carry[8 + k])
        return tuple(carry)

    passed = pass_on(5, arrived)
    passed.wait_recv()
    found = tuple(jnp.zeros((8, LANES), jnp.float32) for _ in range(16))

    def several_totals(step, carry):
        for inner in range(unroll):
            carry = pick_total(step * unroll + inner, carry)
        return carry

    found = lax.fori_loop(0, tiles // unroll, several_totals, found)
    for half, rows in enumerate(halves):
        share, forced = shares[4 * half], [factors[4 * half] * found[4 * half + 8 * part] for part in range(2)]
        for k in range(4 * half + 1, 4 * half + 4):
            share = share + shares[k]
            forced = [forced[part] + factors[k] * found[k + 8 * part] for part in range(2)]
        scale = wet_now[rows] * DT_OCEAN
        for part in range(2):
            ocean_out[part * levels, rows, :] += scale * (forced[part] / share)

    for copy in edges + ocean_edges + edges2:
        copy.wait_send()
    for index, ref, count in ((0, outgoing, tiles - 1), (1, marks, half_tiles - 1), (5, arrived, half_tiles - 1)):
        sent = ref.at[pl.ds(0, count)]
        pltpu.make_async_copy(sent, sent, send_sem.at[index]).wait()
    passed_marks.wait_send()
    passed.wait_send()


def on_device(
    tiles,
    bands,
    ocean_velocity,
    ocean_wet,
    coriolis,
    spectrum,
    group_speed,
    source_matrix,
    moments,
    o2w_rows,
    ocean_to_wave_index,
    o2w_weight,
    w2o_rows,
    wave_to_ocean_index,
    wave_to_ocean_weight,
):
    components, levels, rows, columns = ocean_velocity.shape
    layers = components * levels
    height, width, bins = spectrum.shape
    padded_bins = -(-bins // LANES) * LANES
    angle = (np.arange(NDIR) + 0.5) * (2.0 * math.pi / NDIR)
    wheel = np.zeros((8, padded_bins), np.float32)
    wheel[0, :bins] = np.repeat(np.cos(angle), NFREQ)
    wheel[1, :bins] = np.repeat(np.sin(angle), NFREQ)
    wheel_index = np.zeros((8, padded_bins), np.int32)
    wheel_index[:, :bins] = np.tile(np.arange(NFREQ), NDIR)
    operands = (
        ocean_velocity.reshape(layers, rows, columns),
        ocean_wet,
        coriolis.reshape(1, rows),
        spectrum,
        group_speed.reshape(1, NFREQ),
        source_matrix,
        moments,
        o2w_rows[0, 0].T,
        ocean_to_wave_index,
        o2w_weight,
        w2o_rows[0, 0].T,
        wave_to_ocean_index,
        wave_to_ocean_weight,
        jnp.asarray(wheel),
        jnp.asarray(wheel_index),
    )
    f32, bf16, i32 = jnp.float32, jnp.bfloat16, jnp.int32
    V = pltpu.VMEM
    scratch = [
        V((layers, 32, columns), f32), V((rows, columns), i32), V((1, rows), f32), V((10, 32, bins), f32),
        V((1, NFREQ), f32), V((bins, bins), bf16), V((4, bins), f32),
        V((2, tiles), i32), V((4, height, width), i32), V((4, height, width), i32),
        V((4, rows, columns), i32), V((4, rows, columns), i32), V((8, padded_bins), f32), V((8, padded_bins), i32),
        V((tiles, 4, LANES), f32), V((tiles, 4, LANES), f32), V((tiles, 1, tiles), i32), V((tiles, 4, LANES), f32),
    ]
    scratch += [V((height, bins), f32)] * 8
    scratch += [V((layers, columns), f32)] * 4
    scratch += [V((8, layers * rows), f32)] * 4
    scratch += [
        V((10, 32, bins), f32), V((4, height, 16, bins), f32), V((LANES, bins), f32), V((LANES, bins), bf16), V((LANES, bins), bf16),
        V((8, padded_bins), f32), V((8, padded_bins), f32), V((height, 16, LANES), f32), V((height, 16, LANES), f32),
        V((2, LANES, layers * rows), f32), V((8, LANES), f32), V((LANES, LANES), i32), V((8, height, LANES), i32), V((LANES, padded_bins), f32),
        V((bins, LANES), bf16), V((bins, LANES), bf16),
        pltpu.SemaphoreType.DMA((15,)), pltpu.SemaphoreType.DMA((23,)), pltpu.SemaphoreType.DMA((23,)),
    ]
    far_space = pl.BlockSpec(memory_space=pltpu.HBM)
    near_space = pl.BlockSpec(memory_space=pltpu.VMEM)
    ocean_next, spectrum_next = pl.pallas_call(
        functools.partial(kernel, tiles, bands),
        out_shape=(
            pltpu.VMEM((layers, rows, columns), f32),
            pltpu.VMEM((height, width, bins), f32),
        ),
        in_specs=[far_space] * len(operands),
        out_specs=(near_space, near_space),
        scratch_shapes=scratch,
        compiler_params=pltpu.CompilerParams(
            collective_id=0, has_side_effects=True, vmem_limit_bytes=60 << 20
        ),
        name="coupled_step",
    )(*operands)
    return ocean_next.reshape(ocean_velocity.shape), spectrum_next


def solution(mesh):
    placed = (
        P(None, None, "band", "tile"),
        P("band", "tile"),
        P("band"),
        P("band", "tile", None),
        P(),
        P(),
        P(),
        P("tile", "band", None, None),
        P(None, "band", "tile"),
        P(None, "band", "tile"),
        P("tile", "band", None, None),
        P(None, "band", "tile"),
        P(None, "band", "tile"),
    )
    return jax.shard_map(
        functools.partial(on_device, mesh.shape["tile"], mesh.shape["band"]),
        mesh=mesh,
        in_specs=placed,
        out_specs=(P(None, None, "band", "tile"), P("band", "tile", None)),
        check_vma=False,
    )
```
